128 devices in a mesh: blk: 16 (over x, z_lo, core), dp: 8 (over y, z_hi).
Axes of the slice: x: 4, y: 4, z: 4 (z_hi: 2, z_lo: 2; z = z_hi * 2 + z_lo), core: 2. Of those that a mesh axis runs over, the one named last changes fastest.
Arguments:
- x_in: bfloat16 [196608, 896], P(('blk', 'dp')), may hold values from -6 to 6
- cotangent: bfloat16 [98304, 896], P(('blk', 'dp')), may hold values from -0.059814453 to 0.059814453
- seq_len: int32 [16, 8, 8], P('blk'), may hold values from 36 to 204, as said below
- seq_owner: int32 [16, 8, 8], P('blk'), may hold values from 0 to 7, as said below
- proj_master: float32 [2, 896, 2432], P(None, 'dp', 'blk'), may hold values from -0.1875 to 0.1875
- down_master: float32 [2432, 896], P('blk', 'dp'), may hold values from -0.125 to 0.125
- proj_m: float32 [2, 896, 2432], P(None, 'dp', 'blk'), may hold values from -6 to 6
- proj_v: float32 [2, 896, 2432], P(None, 'dp', 'blk'), may hold values from 0.25 to 4
- down_m: float32 [2432, 896], P('blk', 'dp'), may hold values from -6 to 6
- down_v: float32 [2432, 896], P('blk', 'dp'), may hold values from 0.25 to 4
Outputs:
- mixed: bfloat16 [98304, 896], P(('blk', 'dp'))
- new_proj: float32 [2, 896, 2432], P(None, 'dp', 'blk')
- new_down: float32 [2432, 896], P('blk', 'dp')
- new_proj_m: float32 [2, 896, 2432], P(None, 'dp', 'blk')
- new_proj_v: float32 [2, 896, 2432], P(None, 'dp', 'blk')
- new_down_m: float32 [2432, 896], P('blk', 'dp')
- new_down_v: float32 [2432, 896], P('blk', 'dp')
The draws below stay inside these ranges and needn't reach their ends.
Inputs may be any that keep to these rules, and one draw needn't show every extreme that they name: `seq_len`: row [b, g] lists the token counts of the 8 sequences held by dp index g of blk index b, packed in order from its first row; one device of each blk index fills all 1536 rows; some count equals 204 in every draw; the sequences sent to each dp index of a blk index hold exactly 768 tokens together. Row [b, g] is a permutation of the dp indices: sequence k of dp index g goes to dp index seq_owner[b, g, k] of the same blk index.
All inputs are finite; a program needn't handle non-finite values.
Results may differ from the reference program's by a relative error of at most 0.015.
Values may be sent and summed in bfloat16 or wider, within the bound.
No kernel may reach another device: no remote copies, remote signals or barrier semaphores. Data moves between devices by JAX's collectives and lax.ppermute only.
A program may use at most 128 MiB of HBM per device.

```python
import math
import jax
import jax.numpy as jnp
from jax import lax

D = 896
HIDDEN_SIZE = 2432
OUT_CAP = 768
STEP = 100
IN_CAP = 1536
TOKENS_IN = 196608
TOKENS_OUT = 98304
N_BLK = 16
N_DP = 8


def route_lists(key):
    pair_size = OUT_CAP // N_DP
    shift_unit = pair_size // 8
    key_rows = jax.random.split(jax.random.fold_in(key, 11), N_BLK)
    key_cols = jax.random.split(jax.random.fold_in(key, 12), N_BLK)
    key_owner = jax.random.split(jax.random.fold_in(key, 13), N_BLK * N_DP)
    dev_ids = jnp.arange(N_DP, dtype=jnp.int32)

    def one_row(row_key, col_key):
        order = jax.random.permutation(row_key, N_DP)
        order_cols = jax.random.permutation(col_key, N_DP)
        heavy = (dev_ids == order[0]).astype(jnp.int32)
        light = ((dev_ids == order[1]) | (dev_ids == order[2])).astype(jnp.int32)
        loads = pair_size + pair_size * heavy - pair_size // 2 * light
        tilt = shift_unit * (dev_ids == order_cols[0]).astype(jnp.int32) - shift_unit * (dev_ids == order_cols[1]).astype(jnp.int32)
        diagonal_pos = (dev_ids[:, None] + dev_ids[None, :]) % N_DP
        return loads[:, None] + jnp.take(tilt, diagonal_pos)

    def owner_perm(owner_key):
        return jax.random.permutation(owner_key, N_DP)
    matrix = jax.vmap(one_row)(key_rows, key_cols)
    owners = jax.vmap(owner_perm)(key_owner).reshape(N_BLK, N_DP, N_DP).astype(jnp.int32)
    counts = jnp.take_along_axis(matrix, owners, axis=2)
    return (counts.astype(jnp.int32), owners)


def draw_seq_len(key, part):
    return route_lists(key)[0]


def draw_seq_owner(key, part):
    return route_lists(key)[1]


def shard_levels(rng, extent, cuts, smallest, high):
    level, own = 1.0, jax.random.fold_in(rng, 6)
    for position, blocks in cuts:
        heights = jnp.exp(jax.random.uniform(jax.random.fold_in(own, position), (blocks,), jnp.float32, smallest / len(cuts), high / len(cuts)))
        level = level * jnp.repeat(heights, extent[position] // blocks).reshape([-1 if axis == position else 1 for axis in range(len(extent))])
    return level


def normal_values(rng, dims, spread, bound, cuts=(), kind=jnp.bfloat16):
    result = spread * jax.random.normal(rng, dims, jnp.float32)
    if cuts:
        result = result * shard_levels(rng, dims, cuts, -0.22, 0.18)
    return jnp.clip(result, -bound, bound).astype(kind)


def setup_inputs(seed: int = 0) -> dict:
    splits = jax.random.split(jax.random.key(seed), 11)
    return {
        "x_in": normal_values(splits[0], (TOKENS_IN, D), 1.0, 6.0, ((0, 128),)),
        "cotangent": normal_values(splits[1], (TOKENS_OUT, D), 0.01, 0.059814453, ((0, 128),)),
        "seq_len": draw_seq_len(jax.random.fold_in(splits[10], 71), 0),
        "seq_owner": draw_seq_owner(jax.random.fold_in(splits[10], 71), 0),
        "proj_master": normal_values(splits[4], (2, D, HIDDEN_SIZE), D ** -0.5, 0.1875, ((1, 8), (2, 16)), jnp.float32),
        "down_master": normal_values(splits[5], (HIDDEN_SIZE, D), HIDDEN_SIZE ** -0.5, 0.125, ((0, 16), (1, 8)), jnp.float32),
        "proj_m": normal_values(splits[6], (2, D, HIDDEN_SIZE), 1.0, 6.0, ((1, 8), (2, 16)), jnp.float32),
        "proj_v": jnp.clip(jnp.exp(math.log(4.0) - 2.7725887 * jax.random.uniform(splits[7], (2, D, HIDDEN_SIZE), jnp.float32) ** shard_levels(splits[7], (2, D, HIDDEN_SIZE), ((1, 8), (2, 16)), -0.2, 0.2)), 0.25, 4.0),
        "down_m": normal_values(splits[8], (HIDDEN_SIZE, D), 1.0, 6.0, ((0, 16), (1, 8)), jnp.float32),
        "down_v": jnp.clip(jnp.exp(math.log(4.0) - 2.7725887 * jax.random.uniform(splits[9], (HIDDEN_SIZE, D), jnp.float32) ** shard_levels(splits[9], (HIDDEN_SIZE, D), ((0, 16), (1, 8)), -0.2, 0.2)), 0.25, 4.0),
    }


def rebalance(x_in, seq_len, seq_owner):
    dev_ids = jnp.arange(N_DP, dtype=jnp.int32)
    owner_hot = (seq_owner[:, :, :, None] == dev_ids).astype(jnp.int32)
    starts = jnp.cumsum(seq_len, axis=2) - seq_len
    len_to = lax.optimization_barrier(jnp.sum(seq_len[:, :, :, None] * owner_hot, axis=2))
    start_to = lax.optimization_barrier(jnp.sum(starts[:, :, :, None] * owner_hot, axis=2))
    offsets = jnp.cumsum(len_to, axis=1) - len_to
    offsets_t = jnp.transpose(offsets, (0, 2, 1))
    starts_t = jnp.transpose(start_to, (0, 2, 1))
    row_ids = jnp.arange(OUT_CAP, dtype=jnp.int32)
    source_dev = lax.optimization_barrier(jnp.sum((row_ids[None, None, :, None] >= offsets_t[:, :, None, :]).astype(jnp.int32), axis=3)) - 1
    pick = (source_dev[..., None] == dev_ids).astype(jnp.int32)
    base = lax.optimization_barrier(jnp.sum(pick * offsets_t[:, :, None, :], axis=3))
    begin = lax.optimization_barrier(jnp.sum(pick * starts_t[:, :, None, :], axis=3))
    blk_ids = jnp.arange(N_BLK, dtype=jnp.int32)[:, None, None]
    source_row = ((blk_ids * N_DP + source_dev) * IN_CAP + begin + row_ids - base).astype(jnp.int32)
    return jnp.take(x_in, source_row.reshape(-1), axis=0)

def span_terms(normed, delta, w_proj, w_down):
    gate_val = jnp.dot(normed, w_proj[0], preferred_element_type=jnp.float32)
    up_val = jnp.dot(normed, w_proj[1], preferred_element_type=jnp.float32)
    sigmoid_gate = jax.nn.sigmoid(gate_val)
    silu_gate = gate_val * sigmoid_gate
    hidden = (silu_gate * up_val).astype(jnp.bfloat16)
    branch = jnp.dot(hidden, w_down, preferred_element_type=jnp.float32)
    d_hidden = lax.dot_general(delta, w_down, (((1,), (1,)), ((), ())), preferred_element_type=jnp.float32)
    d_gate = (d_hidden * up_val * sigmoid_gate * (1.0 + gate_val * (1.0 - sigmoid_gate))).astype(jnp.bfloat16)
    d_up = (d_hidden * silu_gate).astype(jnp.bfloat16)
    over_rows = (((0,), (0,)), ((), ()))
    grad_down = lax.dot_general(hidden, delta, over_rows, preferred_element_type=jnp.float32)
    grad_gate = lax.dot_general(normed, d_gate, over_rows, preferred_element_type=jnp.float32)
    grad_up = lax.dot_general(normed, d_up, over_rows, preferred_element_type=jnp.float32)
    return (branch, (jnp.stack([grad_gate, grad_up]), grad_down))

def adam(master, grad, first_moment, second_moment):
    first_new = 0.9 * first_moment + 0.1 * grad
    second_new = 0.95 * second_moment + 0.05 * grad * grad
    first_hat = first_new / (1.0 - 0.9 ** STEP)
    second_hat = second_new / (1.0 - 0.95 ** STEP)
    updated = master - 0.0003 * (first_hat / (jnp.sqrt(second_hat) + 1e-08) + 0.1 * master)
    return (updated, first_new, second_new)

def reference(x_in, cotangent, seq_len, seq_owner, proj_master, down_master, proj_m, proj_v, down_m, down_v):
    tokens = rebalance(x_in, seq_len, seq_owner)
    widened = tokens.astype(jnp.float32)
    scale = lax.rsqrt(lax.optimization_barrier(jnp.mean(widened * widened, axis=1, keepdims=True)) + 1e-06)
    normed = (widened * scale).astype(jnp.bfloat16)
    w_proj = proj_master.astype(jnp.bfloat16)
    w_down = down_master.astype(jnp.bfloat16)
    groups = N_BLK * N_DP
    normed_blocks = normed.reshape(groups, OUT_CAP, D)
    delta_blocks = cotangent.reshape(groups, OUT_CAP, D)

    def one_block(sums, item):
        branch, grads = span_terms(item[0], item[1], w_proj, w_down)
        return ((sums[0] + grads[0], sums[1] + grads[1]), branch)
    start_sums = (jnp.zeros((2, D, HIDDEN_SIZE), jnp.float32), jnp.zeros((HIDDEN_SIZE, D), jnp.float32))
    grad_sums, branches = lax.scan(one_block, start_sums, (normed_blocks, delta_blocks))
    mixed = (widened + branches.reshape(groups * OUT_CAP, D)).astype(jnp.bfloat16)
    new_proj, new_proj_m, new_proj_v = adam(proj_master, grad_sums[0], proj_m, proj_v)
    new_down, new_down_m, new_down_v = adam(down_master, grad_sums[1], down_m, down_v)
    return (mixed, new_proj, new_down, new_proj_m, new_proj_v, new_down_m, new_down_v)
```

```python
import functools

import jax
import jax.numpy as jnp
from jax import lax
from jax.experimental import pallas as pl
from jax.experimental.pallas import tpu as pltpu
from jax.sharding import Mesh, PartitionSpec as P

STEP = 100
AXES = ("x", "zl", "c", "y", "zh")
GROUP = ("x", "zl", "y", "zh")
BF = jnp.bfloat16
F32 = jnp.float32
SLOT = 208
WIN = 256
NT = (((1,), (1,)), ((), ()))
MB = 1024 * 1024


def dot(a, b, dims=(((1,), (0,)), ((), ()))):
    return lax.dot_general(a, b, dims, preferred_element_type=F32)


def iota(shape, dim):
    return lax.broadcasted_iota(jnp.int32, shape, dim)


def adam(master, grad, first_moment, second_moment):
    first_new = 0.9 * first_moment + 0.1 * grad
    second_new = 0.95 * second_moment + 0.05 * grad * grad
    first_hat = first_new / (1.0 - 0.9**STEP)
    second_hat = second_new / (1.0 - 0.95**STEP)
    updated = master - 0.0003 * (first_hat / (jnp.sqrt(second_hat) + 1e-08) + 0.1 * master)
    return (updated, first_new, second_new)


def pack_weights_kernel(proj_ref, down_ref, out_ref):
    d, h = proj_ref.shape[1], proj_ref.shape[2]
    eye = (iota((d, d), 0) == iota((d, d), 1)).astype(BF)
    mats = (
        proj_ref[0].astype(BF),
        proj_ref[1].astype(BF),
        dot(eye, down_ref[...].astype(BF), NT).astype(BF),
    )
    rest = jnp.zeros((d, 128), F32)
    for k, m in enumerate(mats):
        out_ref[:, k * 128 : (k + 1) * 128] = m[:, :128]
        row, col = iota((h, 128), 0), iota((h, 128), 1)
        sel = ((row - 128 == col - 32 * k) & (row >= 128)).astype(BF)
        rest = rest + dot(m, sel)
    out_ref[:, 384:512] = rest.astype(BF)


def pack_weights(proj, down):
    return pl.pallas_call(
        pack_weights_kernel,
        out_shape=jax.ShapeDtypeStruct((proj.shape[1], 512), BF),
        in_specs=[pl.BlockSpec(memory_space=pltpu.VMEM)] * 2,
        out_specs=pl.BlockSpec(memory_space=pltpu.VMEM),
        compiler_params=pltpu.CompilerParams(vmem_limit_bytes=32 * MB),
    )(proj, down)


def pack_tokens_kernel(me_ref, len_ref, own_ref, x_ref, out_ref, start_ref):
    n = len_ref.shape[1]
    rows = x_ref.shape[0]
    me = me_ref[0]
    at = jnp.int32(0)
    for k in range(n):
        start_ref[own_ref[me, k]] = at
        at = at + len_ref[me, k]
    for h in range(n):
        begin = start_ref[h]
        base = pl.multiple_of(jnp.minimum((begin // 16) * 16, rows - WIN), 16)
        sel = (iota((SLOT, WIN), 1) - iota((SLOT, WIN), 0) == begin - base).astype(BF)
        out_ref[h] = dot(sel, x_ref[pl.ds(base, WIN), :]).astype(BF)


def pack_tokens(me, seq_len, seq_owner, x_in):
    n = seq_len.shape[0]
    smem = pl.BlockSpec(memory_space=pltpu.SMEM)
    return pl.pallas_call(
        pack_tokens_kernel,
        out_shape=jax.ShapeDtypeStruct((n, SLOT, x_in.shape[1]), BF),
        in_specs=[smem, smem, smem, pl.BlockSpec(memory_space=pltpu.VMEM)],
        out_specs=pl.BlockSpec(memory_space=pltpu.VMEM),
        scratch_shapes=[pltpu.SMEM((n,), jnp.int32)],
        compiler_params=pltpu.CompilerParams(vmem_limit_bytes=32 * MB),
    )(me, seq_len, seq_owner, x_in)


def unpack_tokens_kernel(me_ref, len_ref, own_ref, slots_ref, out_ref, acc_ref):
    n = len_ref.shape[0]
    rows = out_ref.shape[0]
    me = me_ref[0]
    acc_ref[...] = jnp.zeros_like(acc_ref)
    at = jnp.int32(0)
    for g in range(n):
        count = jnp.int32(0)
        for k in range(n):
            count = count + jnp.where(own_ref[g, k] == me, len_ref[g, k], 0)
        base = pl.multiple_of((at // 16) * 16, 16)
        row, col = iota((WIN, SLOT), 0), iota((WIN, SLOT), 1)
        sel = ((row - col == at - base) & (col < count)).astype(BF)
        acc_ref[pl.ds(base, WIN), :] += dot(sel, slots_ref[g]).astype(BF)
        at = at + count
    out_ref[...] = acc_ref[:rows, :]


def unpack_tokens(me, seq_len, seq_owner, slots, rows):
    smem = pl.BlockSpec(memory_space=pltpu.SMEM)
    d = slots.shape[2]
    return pl.pallas_call(
        unpack_tokens_kernel,
        out_shape=jax.ShapeDtypeStruct((rows, d), BF),
        in_specs=[smem, smem, smem, pl.BlockSpec(memory_space=pltpu.VMEM)],
        out_specs=pl.BlockSpec(memory_space=pltpu.VMEM),
        scratch_shapes=[pltpu.VMEM((rows + WIN, d), BF)],
        compiler_params=pltpu.CompilerParams(vmem_limit_bytes=32 * MB),
    )(me, seq_len, seq_owner, slots)


TB = 256


def layer_kernel(
    tok_a, tok_b, cot_a, cot_b, w_ref, rest_ref, grad_ref, own_ref, part_ref,
    nrm, nrm_t, cot, cot_t, hid, dgate, dup, wg, wu, wd, rest_grad,
):
    step = pl.program_id(0)
    rows, d = tok_a.shape
    total = 2 * rows
    blocks = total // TB

    @pl.when(step == 0)
    def _():
        for half, (t_ref, c_ref) in enumerate(((tok_a, cot_a), (tok_b, cot_b))):
            for i in range(rows // TB):
                at = half * rows + i * TB
                t = t_ref[i * TB : (i + 1) * TB, :].astype(F32)
                scale = lax.rsqrt(jnp.mean(t * t, axis=1, keepdims=True) + 1e-06)
                norm = (t * scale).astype(BF)
                nrm[at : at + TB, :] = norm
                nrm_t[:, at : at + TB] = norm.T
                c = c_ref[i * TB : (i + 1) * TB, :]
                cot[at : at + TB, :] = c
                cot_t[:, at : at + TB] = c.T
        tail = jnp.concatenate([rest_ref[b] for b in range(8)], axis=1)
        row, col = iota((1024, 256), 0), iota((1024, 256), 1)
        for k, dst in enumerate((wg, wu, wd)):
            blk, lane = col // 24, col % 24
            sel = ((row == blk * 128 + 32 * k + lane) & (col < 192)).astype(BF)
            mat = dot(tail, sel).astype(BF)
            if k == 2:
                dst[:, 0:256] = mat
            else:
                dst[...] = mat

    @pl.when(step > 0)
    def _():
        at = pl.multiple_of(step * 256, 256)
        for b in range(2):
            wg[:, b * 128 : (b + 1) * 128] = w_ref[b, :, 0:128]
            wu[:, b * 128 : (b + 1) * 128] = w_ref[b, :, 128:256]
        wd[:, pl.ds(at, 256)] = jnp.concatenate([w_ref[0, :, 256:384], w_ref[1, :, 256:384]], axis=1)

    lanes = pl.ds(pl.multiple_of(step * 256, 256), 256)

    def body(i, _):
        at = pl.ds(pl.multiple_of(i * TB, TB), TB)
        n = nrm[at, :]
        g = dot(n, wg[...])
        u = dot(n, wu[...])
        dh = dot(cot[at, :], wd[:, lanes])
        s = 0.5 * jnp.tanh(0.5 * g) + 0.5
        silu = g * s
        hid[at, lanes] = (silu * u).astype(BF)
        dgate[at, :] = (dh * u * s * (1.0 + g * (1.0 - s))).astype(BF)
        dup[at, :] = (dh * silu).astype(BF)
        return 0

    lax.fori_loop(0, blocks, body, 0)
    g_gate = dot(nrm_t[...], dgate[...]).astype(BF)
    g_up = dot(nrm_t[...], dup[...]).astype(BF)
    g_down = dot(cot_t[...], hid[:, lanes]).astype(BF)

    @pl.when(step == 0)
    def _():
        col, row = iota((256, 1024), 1), iota((256, 1024), 0)
        out = jnp.zeros((d, 1024), F32)
        for k, g in enumerate((g_gate, g_up, g_down)):
            sel = ((col == (row // 24) * 128 + 32 * k + row % 24) & (row < 192)).astype(BF)
            out = out + dot(g, sel)
        rest_grad[...] = out.astype(BF)

    @pl.when(step > 0)
    def _():
        at = pl.multiple_of((step - 1) * 256, 256)
        tail = rest_grad[:, pl.ds(at, 256)]
        for b in range(2):
            half = slice(b * 128, (b + 1) * 128)
            grad_ref[b, :, 0:128] = g_gate[:, half]
            grad_ref[b, :, 128:256] = g_up[:, half]
            grad_ref[b, :, 256:384] = g_down[:, half]
            grad_ref[b, :, 384:512] = tail[:, half]

    @pl.when(step == pl.num_programs(0) - 1)
    def _():
        for i in range(rows // TB):
            at = slice(i * TB, (i + 1) * TB)
            own_ref[at, :] = dot(hid[at, :], wd[...], NT) + tok_a[at, :].astype(F32)
            far = slice(rows + i * TB, rows + (i + 1) * TB)
            part_ref[at, :] = dot(hid[far, :], wd[...], NT).astype(BF)


def layer(tok_a, tok_b, cot_a, cot_b, w):
    rows, d = tok_a.shape
    whole = lambda a: pl.BlockSpec(a.shape, lambda j: (0,) * a.ndim)
    total = 2 * rows
    return pl.pallas_call(
        layer_kernel,
        grid=(5,),
        out_shape=(
            jax.ShapeDtypeStruct((8, d, 512), BF),
            jax.ShapeDtypeStruct((rows, d), F32),
            jax.ShapeDtypeStruct((rows, d), BF),
        ),
        in_specs=[
            whole(tok_a),
            whole(tok_b),
            whole(cot_a),
            whole(cot_b),
            pl.BlockSpec((2, d, 384), lambda j: (jnp.maximum(j - 1, 0), 0, 0)),
            pl.BlockSpec((8, d, 128), lambda j: (0, 0, 3)),
        ],
        out_specs=(
            pl.BlockSpec((2, d, 512), lambda j: (jnp.maximum(j - 1, 0), 0, 0)),
            pl.BlockSpec((rows, d), lambda j: (0, 0)),
            pl.BlockSpec((rows, d), lambda j: (0, 0)),
        ),
        scratch_shapes=[
            pltpu.VMEM((total, d), BF),
            pltpu.VMEM((d, total), BF),
            pltpu.VMEM((total, d), BF),
            pltpu.VMEM((d, total), BF),
            pltpu.VMEM((total, 1280), BF),
            pltpu.VMEM((total, 256), BF),
            pltpu.VMEM((total, 256), BF),
            pltpu.VMEM((d, 256), BF),
            pltpu.VMEM((d, 256), BF),
            pltpu.VMEM((d, 1280), BF),
            pltpu.VMEM((d, 1024), BF),
        ],
        compiler_params=pltpu.CompilerParams(vmem_limit_bytes=60 * MB),
        cost_estimate=pl.CostEstimate(flops=25_000_000_000, bytes_accessed=30_000_000, transcendentals=2_000_000),
    )(tok_a, tok_b, cot_a, cot_b, w, w)


def swap_cores(v):
    return lax.ppermute(v, "c", [(0, 1), (1, 0)])


def per_device(
    x_in, cotangent, seq_len, seq_owner, proj_master, down_master, proj_m, proj_v, down_m, down_v
):
    rows, d = cotangent.shape
    me = (lax.axis_index("y") * lax.axis_size("zh") + lax.axis_index("zh")).reshape(1)
    counts, owners = seq_len[0], seq_owner[0]
    slots = pack_tokens(me, counts, owners, x_in)
    packed = pack_weights(proj_master, down_master)
    slots = lax.all_to_all(slots, ("y", "zh"), 0, 0, tiled=True)
    cot_b = swap_cores(cotangent)
    w = lax.all_to_all(
        jnp.broadcast_to(packed[None], (64,) + packed.shape), GROUP, 0, 0, tiled=True
    )
    tok_a = unpack_tokens(me, counts, owners, slots, rows)
    tok_b = swap_cores(tok_a)
    grads, own, part = layer(tok_a, tok_b, cotangent, cot_b, w.reshape(8, d, 512))
    mixed = (own + swap_cores(part).astype(F32)).astype(BF)
    pieces = lax.all_to_all(grads.reshape(64, d // 8, 512), GROUP, 0, 0, tiled=True)
    total = jnp.sum(pieces.astype(F32), axis=0)
    g_gate = jnp.concatenate([total[:, 0:128], total[:, 384:408]], axis=1)
    g_up = jnp.concatenate([total[:, 128:256], total[:, 416:440]], axis=1)
    g_down = jnp.concatenate([total[:, 256:384], total[:, 448:472]], axis=1).T
    new_proj, new_proj_m, new_proj_v = adam(proj_master, jnp.stack([g_gate, g_up]), proj_m, proj_v)
    new_down, new_down_m, new_down_v = adam(down_master, g_down, down_m, down_v)
    return (mixed, new_proj, new_down, new_proj_m, new_proj_v, new_down_m, new_down_v)


def solution(mesh):
    mesh = Mesh(mesh.devices.reshape(4, 2, 2, 4, 2), AXES)
    blk, dp = ("x", "zl", "c"), ("y", "zh")
    in_specs = (
        P(blk + dp, None),
        P(blk + dp, None),
        P(blk, None, None),
        P(blk, None, None),
        P(None, dp, blk),
        P(blk, dp),
        P(None, dp, blk),
        P(None, dp, blk),
        P(blk, dp),
        P(blk, dp),
    )
    out_specs = (
        P(blk + dp, None),
        P(None, dp, blk),
        P(blk, dp),
        P(None, dp, blk),
        P(None, dp, blk),
        P(blk, dp),
        P(blk, dp),
    )
    return jax.shard_map(
        per_device, mesh=mesh, in_specs=in_specs, out_specs=out_specs, check_vma=False
    )
```

```python
import jax
import jax.numpy as jnp
from jax import lax
from jax.experimental import pallas as pl
from jax.experimental.pallas import tpu as pltpu
from jax.sharding import Mesh, PartitionSpec as P

STEP = 100
AXES = ("x", "zl", "c", "y", "zh")
GROUP = ("x", "zl", "y", "zh")
BF = jnp.bfloat16
F32 = jnp.float32
SLOT = 208
WIN = 256
NT = (((1,), (1,)), ((), ()))
MB = 1024 * 1024
SIZE = (12, 12, 14)
LANE = (0, 36, 72)
UNIT = (0, 48, 96)
ROWS = tuple(8 * n for n in SIZE)
PART = sum(ROWS)
FIRST = (0, ROWS[0], ROWS[0] + ROWS[1])
HOPS = (1, -1, 2)


def dot(a, b, dims=(((1,), (0,)), ((), ()))):
    return lax.dot_general(a, b, dims, preferred_element_type=F32)


def iota(shape, dim):
    return lax.broadcasted_iota(jnp.int32, shape, dim)


def adam(master, grad, first_moment, second_moment):
    first_new = 0.9 * first_moment + 0.1 * grad
    second_new = 0.95 * second_moment + 0.05 * grad * grad
    first_hat = first_new / (1.0 - 0.9**STEP)
    second_hat = second_new / (1.0 - 0.95**STEP)
    updated = master - 0.0003 * (first_hat / (jnp.sqrt(second_hat) + 1e-08) + 0.1 * master)
    return (updated, first_new, second_new)


def pack_tokens_kernel(me_ref, len_ref, own_ref, x_ref, out_ref, start_ref):
    n = len_ref.shape[1]
    rows = x_ref.shape[0]
    me = me_ref[0]
    at = jnp.int32(0)
    for k in range(n):
        start_ref[own_ref[me, k]] = at
        at = at + len_ref[me, k]
    for h in range(n):
        begin = start_ref[h]
        base = pl.multiple_of(jnp.minimum((begin // 16) * 16, rows - WIN), 16)
        sel = (iota((SLOT, WIN), 1) - iota((SLOT, WIN), 0) == begin - base).astype(BF)
        out_ref[h] = dot(sel, x_ref[pl.ds(base, WIN), :]).astype(BF)


def pack_tokens(me, seq_len, seq_owner, x_in):
    n = seq_len.shape[0]
    smem = pl.BlockSpec(memory_space=pltpu.SMEM)
    return pl.pallas_call(
        pack_tokens_kernel,
        out_shape=jax.ShapeDtypeStruct((n, SLOT, x_in.shape[1]), BF),
        in_specs=[smem, smem, smem, pl.BlockSpec(memory_space=pltpu.VMEM)],
        out_specs=pl.BlockSpec(memory_space=pltpu.VMEM),
        scratch_shapes=[pltpu.SMEM((n,), jnp.int32)],
        compiler_params=pltpu.CompilerParams(vmem_limit_bytes=32 * MB),
    )(me, seq_len, seq_owner, x_in)


def unpack_tokens_kernel(me_ref, len_ref, own_ref, slots_ref, out_ref, acc_ref):
    n = len_ref.shape[0]
    rows = out_ref.shape[0]
    me = me_ref[0]
    acc_ref[...] = jnp.zeros_like(acc_ref)
    at = jnp.int32(0)
    for g in range(n):
        count = jnp.int32(0)
        for k in range(n):
            count = count + jnp.where(own_ref[g, k] == me, len_ref[g, k], 0)
        base = pl.multiple_of((at // 16) * 16, 16)
        row, col = iota((WIN, SLOT), 0), iota((WIN, SLOT), 1)
        sel = ((row - col == at - base) & (col < count)).astype(BF)
        acc_ref[pl.ds(base, WIN), :] += dot(sel, slots_ref[g]).astype(BF)
        at = at + count
    out_ref[...] = acc_ref[:rows, :]


def unpack_tokens(me, seq_len, seq_owner, slots, rows):
    smem = pl.BlockSpec(memory_space=pltpu.SMEM)
    d = slots.shape[2]
    return pl.pallas_call(
        unpack_tokens_kernel,
        out_shape=jax.ShapeDtypeStruct((rows, d), BF),
        in_specs=[smem, smem, smem, pl.BlockSpec(memory_space=pltpu.VMEM)],
        out_specs=pl.BlockSpec(memory_space=pltpu.VMEM),
        scratch_shapes=[pltpu.VMEM((rows + WIN, d), BF)],
        compiler_params=pltpu.CompilerParams(vmem_limit_bytes=32 * MB),
    )(me, seq_len, seq_owner, slots)


VMEM = pl.BlockSpec(memory_space=pltpu.VMEM)


def params(size):
    return pltpu.CompilerParams(vmem_limit_bytes=size * MB)


def by_stream(index, values):
    out = jnp.full(index.shape, values[0], jnp.int32)
    for s in (1, 2):
        out = jnp.where(index == s, values[s], out)
    return out


def place(matrix, shape, unit_dim):
    col, unit = iota(shape, 1 - unit_dim), iota(shape, unit_dim)
    stream, part, lane = col // 512, (col // 128) % 4, col % 128
    size = by_stream(stream, SIZE)
    i = lane - by_stream(stream, LANE) - matrix * size
    return (i >= 0) & (i < size) & (unit == by_stream(stream, UNIT) + size * part + i)


def assemble(shape, row_dim):
    row, col = iota(shape, row_dim), iota(shape, 1 - row_dim)
    stream = (row >= 3 * FIRST[1]).astype(jnp.int32) + (row >= 3 * FIRST[2]).astype(jnp.int32)
    local = row - 3 * by_stream(stream, FIRST)
    size = by_stream(stream, SIZE)
    matrix = (local >= 8 * size).astype(jnp.int32) + (local >= 16 * size).astype(jnp.int32)
    local = local - matrix * 8 * size
    blk, lane = col // 128, col % 128
    i = lane - by_stream(stream, LANE) - matrix * size
    return (i >= 0) & (i < size) & (local == blk * size + i) & (row < 3 * PART)


def pack_weights_kernel(proj_ref, down_ref, out_ref):
    h, d = down_ref.shape
    eye = (iota((d, d), 0) == iota((d, d), 1)).astype(BF)
    total = jnp.zeros((d, 1536), F32)
    for k in range(3):
        m = (down_ref[...] if k == 2 else proj_ref[k]).astype(BF)
        turned = dot(eye, m, NT).astype(BF)
        total = total + dot(turned, place(k, (h, 1536), 0).astype(BF))
    total = total.astype(BF)
    at = lambda s, p: total[:, s * 512 + p * 128 : s * 512 + (p + 1) * 128]
    for x in range(4):
        for zl in range(2):
            for y in range(4):
                for zh in range(2):
                    index = ((x * 2 + zl) * 4 + y) * 2 + zh
                    out_ref[index] = at(0, x) + at(1, y) + at(2, zh * 2 + zl)


def pack_weights(proj, down):
    return pl.pallas_call(
        pack_weights_kernel,
        out_shape=jax.ShapeDtypeStruct((64, down.shape[1], 128), BF),
        in_specs=[VMEM] * 2,
        out_specs=VMEM,
        compiler_params=params(24),
    )(proj, down)


def assemble_kernel(a_ref, *out_refs):
    d = a_ref.shape[1]
    wide = jnp.concatenate([a_ref[b] for b in range(8)], axis=1)
    for s, out in enumerate(out_refs):
        n = 3 * ROWS[s]
        sel = assemble((3 * PART, 1024), 0)[3 * FIRST[s] : 3 * FIRST[s] + n].astype(F32).astype(BF)
        out[...] = dot(sel, wide, NT).astype(BF)


def assemble_weights(a):
    d = a.shape[1]
    return pl.pallas_call(
        assemble_kernel,
        out_shape=tuple(jax.ShapeDtypeStruct((3 * n, d), BF) for n in ROWS),
        in_specs=[VMEM],
        out_specs=(VMEM,) * 3,
        compiler_params=params(24),
    )(a)


TB = 256


def turn_kernel(a_ref, b_ref, out_ref, turned_ref, *, normalise):
    rows = a_ref.shape[0]
    for half, ref in enumerate((a_ref, b_ref)):
        for i in range(rows // TB):
            at = half * rows + i * TB
            t = ref[i * TB : (i + 1) * TB, :]
            if normalise:
                t = t.astype(F32)
                scale = lax.rsqrt(jnp.mean(t * t, axis=1, keepdims=True) + 1e-06)
                t = (t * scale).astype(BF)
            out_ref[at : at + TB, :] = t
            turned_ref[:, at : at + TB] = t.T


def turn(a, b, normalise):
    rows, d = a.shape
    return pl.pallas_call(
        lambda *refs: turn_kernel(*refs, normalise=normalise),
        out_shape=(
            jax.ShapeDtypeStruct((2 * rows, d), BF),
            jax.ShapeDtypeStruct((d, 2 * rows), BF),
        ),
        in_specs=[VMEM] * 2,
        out_specs=(VMEM,) * 2,
        compiler_params=params(24),
    )(a, b)


def part_kernel(
    nrm, nrm_t, cot, cot_t, wx, wy, wz, gx, gy, gz, hid, w, back,
):
    total = nrm.shape[0]
    for s, src in enumerate((wx, wy, wz)):
        n = ROWS[s]
        for m in range(3):
            w[m * PART + FIRST[s] : m * PART + FIRST[s] + n, :] = src[m * n : (m + 1) * n, :]

    def body(i, _):
        at = pl.ds(pl.multiple_of(i * TB, TB), TB)
        gu = dot(w[: 2 * PART, :], nrm_t[:, at])
        dh = dot(w[2 * PART :, :], cot_t[:, at])
        g, u = gu[:PART], gu[PART:]
        s = 0.5 * jnp.tanh(0.5 * g) + 0.5
        silu = g * s
        h = (silu * u).astype(BF)
        back[:PART, at] = (dh * u * s * (1.0 + g * (1.0 - s))).astype(BF)
        back[PART : 2 * PART, at] = (dh * silu).astype(BF)
        back[2 * PART :, at] = h
        hid[:, at] = h
        return 0

    lax.fori_loop(0, total // TB, body, 0)
    w[: 2 * PART, :] = dot(back[: 2 * PART, :], nrm[...]).astype(BF)
    w[2 * PART :, :] = dot(back[2 * PART :, :], cot[...]).astype(BF)
    for s, dst in enumerate((gx, gy, gz)):
        n = ROWS[s]
        for m in range(3):
            dst[m * n : (m + 1) * n, :] = w[m * PART + FIRST[s] : m * PART + FIRST[s] + n, :]


def one_part(nrm, nrm_t, cot, cot_t, weights):
    total, d = nrm.shape
    out = pl.pallas_call(
        part_kernel,
        out_shape=tuple(jax.ShapeDtypeStruct((3 * n, d), BF) for n in ROWS)
        + (jax.ShapeDtypeStruct((PART, total), BF),),
        in_specs=[VMEM] * 7,
        out_specs=(VMEM,) * 4,
        scratch_shapes=[pltpu.VMEM((3 * PART, d), BF), pltpu.VMEM((3 * PART, total), BF)],
        compiler_params=params(34),
        cost_estimate=pl.CostEstimate(
            flops=6_000_000_000, bytes_accessed=16_000_000, transcendentals=500_000
        ),
    )(nrm, nrm_t, cot, cot_t, *weights)
    return out[:3], out[3]


def mix_kernel(tok_ref, *refs):
    hids, weights, (own_ref, far_ref) = refs[:4], refs[4:16], refs[16:]
    rows = tok_ref.shape[0]
    for i in range(2 * rows // TB):
        at = slice(i * TB, (i + 1) * TB)
        total = None
        for k in range(4):
            h = hids[k][:, at].T
            for s in range(3):
                n = ROWS[s]
                part = dot(h[:, FIRST[s] : FIRST[s] + n], weights[3 * k + s][2 * n : 3 * n, :])
                total = part if total is None else total + part
        if i * TB < rows:
            own_ref[at, :] = total + tok_ref[at, :].astype(F32)
        else:
            far_ref[i * TB - rows : (i + 1) * TB - rows, :] = total.astype(BF)


def mix(tok, hids, weights):
    rows, d = tok.shape
    return pl.pallas_call(
        mix_kernel,
        out_shape=(jax.ShapeDtypeStruct((rows, d), F32), jax.ShapeDtypeStruct((rows, d), BF)),
        in_specs=[VMEM] * 17,
        out_specs=(VMEM,) * 2,
        compiler_params=params(34),
        cost_estimate=pl.CostEstimate(
            flops=3_500_000_000, bytes_accessed=16_000_000, transcendentals=0
        ),
    )(tok, *hids, *[w for part in weights for w in part])


def pack_grads_kernel(*refs):
    out_ref, rows_ref = refs[12], refs[13]
    d = out_ref.shape[1]
    for s in range(3):
        total = refs[s][...].astype(F32)
        for k in range(1, 4):
            total = total + refs[3 * k + s][...].astype(F32)
        rows_ref[3 * FIRST[s] : 3 * FIRST[s] + 3 * ROWS[s], :] = total.astype(BF)
    rows_ref[3 * PART :, :] = jnp.zeros((1024 - 3 * PART, d), BF)
    turned = rows_ref[...].T
    for b in range(8):
        sel = assemble((1024, 1024), 0)[:, b * 128 : (b + 1) * 128].astype(F32).astype(BF)
        out_ref[b] = dot(turned, sel).astype(BF)


def pack_grads(parts):
    d = parts[0][0].shape[1]
    return pl.pallas_call(
        pack_grads_kernel,
        out_shape=jax.ShapeDtypeStruct((8, d, 128), BF),
        in_specs=[VMEM] * 12,
        out_specs=VMEM,
        scratch_shapes=[pltpu.VMEM((1024, d), BF)],
        compiler_params=params(40),
    )(*[g for part in parts for g in part])


def update_kernel(a_ref, *refs):
    (proj, proj_m, proj_v, down, down_m, down_v), outs = refs[:6], refs[6:]
    h, d = down.shape
    sums = [[None] * 4 for _ in range(3)]
    for x in range(4):
        for zl in range(2):
            for y in range(4):
                for zh in range(2):
                    v = a_ref[((x * 2 + zl) * 4 + y) * 2 + zh].astype(F32)
                    for s, p in enumerate((x, y, zh * 2 + zl)):
                        sums[s][p] = v if sums[s][p] is None else sums[s][p] + v
    wide = jnp.concatenate([v for part in sums for v in part], axis=1)
    high = wide.astype(BF)
    low = (wide - high.astype(F32)).astype(BF)
    for k in range(3):
        sel = place(k, (h, 1536), 0).astype(BF)
        grad = dot(sel, high, NT) + dot(sel, low, NT)
        if k < 2:
            new = adam(proj[k], grad, proj_m[k], proj_v[k])
            for out, v in zip(outs[:3], new):
                out[k] = v
        else:
            new = adam(down[...], grad, down_m[...], down_v[...])
            for out, v in zip(outs[3:], new):
                out[...] = v


def update(pieces, proj, proj_m, proj_v, down, down_m, down_v):
    shape = lambda a: jax.ShapeDtypeStruct(a.shape, F32)
    return pl.pallas_call(
        update_kernel,
        out_shape=(shape(proj),) * 3 + (shape(down),) * 3,
        in_specs=[VMEM] * 7,
        out_specs=(VMEM,) * 6,
        compiler_params=params(24),
    )(pieces, proj, proj_m, proj_v, down, down_m, down_v)


def shift_pairs(sizes, axis, hops):
    pairs = []
    nx, nzl, nc, ny, nzh = sizes
    line = lambda x, zl, c, y, zh: (((x * nzl + zl) * nc + c) * ny + y) * nzh + zh
    for x in range(nx):
        for zl in range(nzl):
            for c in range(nc):
                for y in range(ny):
                    for zh in range(nzh):
                        to = [x, y, zh * nzl + zl]
                        to[axis] = (to[axis] + hops) % (nx, ny, nzh * nzl)[axis]
                        pairs.append(
                            (
                                line(x, zl, c, y, zh),
                                line(to[0], to[2] % nzl, c, to[1], to[2] // nzl),
                            )
                        )
    return pairs


def shifted(parts, hops):
    sizes = tuple(lax.axis_size(a) for a in AXES)
    return tuple(
        lax.ppermute(v, AXES, shift_pairs(sizes, axis, hops)) for axis, v in enumerate(parts)
    )


def swap_cores(v):
    return lax.ppermute(v, "c", [(0, 1), (1, 0)])


def per_device(
    x_in, cotangent, seq_len, seq_owner, proj_master, down_master, proj_m, proj_v, down_m, down_v
):
    rows, d = cotangent.shape
    me = (lax.axis_index("y") * lax.axis_size("zh") + lax.axis_index("zh")).reshape(1)
    counts, owners = seq_len[0], seq_owner[0]
    flip = lambda v: jnp.swapaxes(v, 1, 2)
    slots = pack_tokens(me, counts, owners, x_in)
    slots = lax.all_to_all(slots, ("y", "zh"), 0, 0, tiled=True)
    packed = pack_weights(flip(proj_master), down_master)
    cot, cot_t = turn(cotangent, swap_cores(cotangent), False)
    arrived = lax.all_to_all(packed, GROUP, 0, 0, tiled=True)
    tok_a = unpack_tokens(me, counts, owners, slots, rows)
    nrm, nrm_t = turn(tok_a, swap_cores(tok_a), True)
    own = assemble_weights(arrived.reshape(8, d, 128))
    weights = [shifted(own, -k) for k in HOPS] + [own]
    grads, hids = [], []
    for w in weights:
        g, h = one_part(nrm, nrm_t, cot, cot_t, w)
        grads.append(g)
        hids.append(h)
    sums = [shifted(g, k) for g, k in zip(grads, HOPS)] + [grads[3]]
    messages = pack_grads(sums).reshape(64, d // 8, 128)
    pieces = lax.all_to_all(messages, GROUP, 0, 0, tiled=True)
    near, far = mix(tok_a, hids, weights)
    mixed = (near + swap_cores(far).astype(F32)).astype(BF)
    out = update(
        pieces, flip(proj_master), flip(proj_m), flip(proj_v), down_master, down_m, down_v
    )
    new_proj, new_proj_m, new_proj_v = (flip(v) for v in out[:3])
    new_down, new_down_m, new_down_v = out[3:]
    return (mixed, new_proj, new_down, new_proj_m, new_proj_v, new_down_m, new_down_v)


def solution(mesh):
    mesh = Mesh(mesh.devices.reshape(4, 2, 2, 4, 2), AXES)
    blk, dp = ("x", "zl", "c"), ("y", "zh")
    in_specs = (
        P(blk + dp, None),
        P(blk + dp, None),
        P(blk, None, None),
        P(blk, None, None),
        P(None, dp, blk),
        P(blk, dp),
        P(None, dp, blk),
        P(None, dp, blk),
        P(blk, dp),
        P(blk, dp),
    )
    out_specs = (
        P(blk + dp, None),
        P(None, dp, blk),
        P(blk, dp),
        P(None, dp, blk),
        P(None, dp, blk),
        P(blk, dp),
        P(blk, dp),
    )
    return jax.shard_map(
        per_device, mesh=mesh, in_specs=in_specs, out_specs=out_specs, check_vma=False
    )
```

```python
import jax
import jax.numpy as jnp
from jax import lax
from jax.experimental import pallas as pl
from jax.experimental.pallas import tpu as pltpu
from jax.sharding import Mesh, PartitionSpec as P

STEP = 100
AXES = ("x", "zl", "c", "y", "zh")
GROUP = ("x", "zl", "y", "zh")
BF = jnp.bfloat16
F32 = jnp.float32
SLOT = 208
WIN = 256
NT = (((1,), (1,)), ((), ()))
MB = 1024 * 1024
SIZE = (12, 12, 14)
LANE = (0, 36, 72)
UNIT = (0, 48, 96)
ROWS = tuple(8 * n for n in SIZE)
PART = sum(ROWS)
FIRST = (0, ROWS[0], ROWS[0] + ROWS[1])
HOPS = (2, -1, 1)


def dot(a, b, dims=(((1,), (0,)), ((), ()))):
    return lax.dot_general(a, b, dims, preferred_element_type=F32)


def iota(shape, dim):
    return lax.broadcasted_iota(jnp.int32, shape, dim)


def adam(master, grad, first_moment, second_moment):
    first_new = 0.9 * first_moment + 0.1 * grad
    second_new = 0.95 * second_moment + 0.05 * grad * grad
    first_hat = first_new / (1.0 - 0.9**STEP)
    second_hat = second_new / (1.0 - 0.95**STEP)
    updated = master - 0.0003 * (first_hat / (jnp.sqrt(second_hat) + 1e-08) + 0.1 * master)
    return (updated, first_new, second_new)


VMEM = pl.BlockSpec(memory_space=pltpu.VMEM)
SMEM = pl.BlockSpec(memory_space=pltpu.SMEM)
ANY = pl.BlockSpec(memory_space=pl.ANY)
TB = 256


def params(size):
    return pltpu.CompilerParams(vmem_limit_bytes=size * MB)


def by_stream(index, values):
    out = jnp.full(index.shape, values[0], jnp.int32)
    for s in (1, 2):
        out = jnp.where(index == s, values[s], out)
    return out


def place(matrix, shape, unit_dim):
    col, unit = iota(shape, 1 - unit_dim), iota(shape, unit_dim)
    stream, part, lane = col // 512, (col // 128) % 4, col % 128
    size = by_stream(stream, SIZE)
    i = lane - by_stream(stream, LANE) - matrix * size
    return (i >= 0) & (i < size) & (unit == by_stream(stream, UNIT) + size * part + i)


def assemble(shape, row_dim):
    row, col = iota(shape, row_dim), iota(shape, 1 - row_dim)
    stream = (row >= 3 * FIRST[1]).astype(jnp.int32) + (row >= 3 * FIRST[2]).astype(jnp.int32)
    local = row - 3 * by_stream(stream, FIRST)
    size = by_stream(stream, SIZE)
    matrix = (local >= 8 * size).astype(jnp.int32) + (local >= 16 * size).astype(jnp.int32)
    local = local - matrix * 8 * size
    blk, lane = col // 128, col % 128
    i = lane - by_stream(stream, LANE) - matrix * size
    return (i >= 0) & (i < size) & (local == blk * size + i) & (row < 3 * PART)


def pack_kernel(
    me_ref, len_ref, own_ref, x_ref, proj_ref, down_ref, slots_ref, out_ref,
    rows_ref, proj, down, slots, lens, owns, starts, sems, out_sems,
):
    pairs = (
        (proj_ref, proj), (down_ref, down), (len_ref, lens), (own_ref, owns), (x_ref, rows_ref),
    )
    copies = [pltpu.make_async_copy(a, b, sems.at[k]) for k, (a, b) in enumerate(pairs)]
    for copy in copies:
        copy.start()
    h, d = down.shape
    eye = (iota((d, d), 0) == iota((d, d), 1)).astype(BF)
    total = jnp.zeros((d, 1536), F32)
    copies[0].wait()
    copies[1].wait()
    for k in range(3):
        m = (down[...] if k == 2 else proj[k]).astype(BF)
        turned = dot(eye, m, NT).astype(BF)
        total = total + dot(turned, place(k, (h, 1536), 0).astype(BF))
    total = total.astype(BF)
    at = lambda s, p: total[:, s * 512 + p * 128 : s * 512 + (p + 1) * 128]
    for x in range(4):
        for zl in range(2):
            for y in range(4):
                for zh in range(2):
                    index = ((x * 2 + zl) * 4 + y) * 2 + zh
                    out_ref[index] = at(0, x) + at(1, y) + at(2, zh * 2 + zl)
    copies[2].wait()
    copies[3].wait()
    n = lens.shape[1]
    rows = rows_ref.shape[0]
    me = me_ref[0]
    first = jnp.int32(0)
    for k in range(n):
        starts[owns[me, k]] = first
        first = first + lens[me, k]
    copies[4].wait()
    sent = []
    for g in range(n):
        begin = starts[g]
        base = pl.multiple_of(jnp.minimum((begin // 16) * 16, rows - WIN), 16)
        sel = (iota((SLOT, WIN), 1) - iota((SLOT, WIN), 0) == begin - base).astype(BF)
        slots[g] = dot(sel, rows_ref[pl.ds(base, WIN), :]).astype(BF)
        sent.append(pltpu.make_async_copy(slots.at[g], slots_ref.at[g], out_sems.at[g]))
        sent[-1].start()
    for copy in sent:
        copy.wait()


def pack(me, seq_len, seq_owner, x_in, proj, down):
    n = seq_len.shape[0]
    slots = (n, SLOT, x_in.shape[1])
    return pl.pallas_call(
        pack_kernel,
        out_shape=(
            jax.ShapeDtypeStruct(slots, BF),
            jax.ShapeDtypeStruct((64, down.shape[1], 128), BF),
        ),
        in_specs=[SMEM, ANY, ANY, ANY, ANY, ANY],
        out_specs=(ANY, VMEM),
        scratch_shapes=[
            pltpu.VMEM(x_in.shape, BF),
            pltpu.VMEM(proj.shape, F32),
            pltpu.VMEM(down.shape, F32),
            pltpu.VMEM(slots, BF),
            pltpu.SMEM((n, n), jnp.int32),
            pltpu.SMEM((n, n), jnp.int32),
            pltpu.SMEM((n,), jnp.int32),
            pltpu.SemaphoreType.DMA((5,)),
            pltpu.SemaphoreType.DMA((n,)),
        ],
        compiler_params=params(58),
    )(me, seq_len, seq_owner, x_in, proj, down)


def unpack_kernel(me_ref, len_ref, own_ref, slots_ref, cot_ref, after_ref, out_ref, acc_ref):
    n = len_ref.shape[0]
    rows = out_ref.shape[1]
    me = me_ref[0]
    acc_ref[...] = jnp.zeros_like(acc_ref)
    at = jnp.int32(0)
    for g in range(n):
        count = jnp.int32(0)
        for k in range(n):
            count = count + jnp.where(own_ref[g, k] == me, len_ref[g, k], 0)
        base = pl.multiple_of((at // 16) * 16, 16)
        row, col = iota((WIN, SLOT), 0), iota((WIN, SLOT), 1)
        sel = ((row - col == at - base) & (col < count)).astype(BF)
        acc_ref[pl.ds(base, WIN), :] += dot(sel, slots_ref[g]).astype(BF)
        at = at + count
    out_ref[0] = acc_ref[:rows, :]
    out_ref[1] = cot_ref[...]


def unpack(me, seq_len, seq_owner, slots, cot, after):
    rows, d = cot.shape
    return pl.pallas_call(
        unpack_kernel,
        out_shape=jax.ShapeDtypeStruct((2, rows, d), BF),
        in_specs=[SMEM, SMEM, SMEM, VMEM, VMEM, ANY],
        out_specs=VMEM,
        scratch_shapes=[pltpu.VMEM((rows + WIN, d), BF)],
        compiler_params=params(24),
    )(me, seq_len, seq_owner, slots, cot, after)


def turn_kernel(a_ref, b_ref, nrm_ref, nrm_t_ref, cot_ref, cot_t_ref):
    rows = a_ref.shape[1]
    for half, ref in enumerate((a_ref, b_ref)):
        for i in range(rows // TB):
            at = half * rows + i * TB
            t = ref[0, i * TB : (i + 1) * TB, :].astype(F32)
            scale = lax.rsqrt(jnp.mean(t * t, axis=1, keepdims=True) + 1e-06)
            t = (t * scale).astype(BF)
            nrm_ref[at : at + TB, :] = t
            nrm_t_ref[:, at : at + TB] = t.T
            c = ref[1, i * TB : (i + 1) * TB, :]
            cot_ref[at : at + TB, :] = c
            cot_t_ref[:, at : at + TB] = c.T


def turn(a, b):
    _, rows, d = a.shape
    flat, turned = jax.ShapeDtypeStruct((2 * rows, d), BF), jax.ShapeDtypeStruct((d, 2 * rows), BF)
    return pl.pallas_call(
        turn_kernel,
        out_shape=(flat, turned, flat, turned),
        in_specs=[VMEM] * 2,
        out_specs=(VMEM,) * 4,
        compiler_params=params(30),
    )(a, b)


def assemble_kernel(a_ref, *out_refs):
    d = a_ref.shape[1]
    wide = jnp.concatenate([a_ref[b] for b in range(8)], axis=1)
    for s, out in enumerate(out_refs):
        n = 3 * ROWS[s]
        sel = assemble((3 * PART, 1024), 0)[3 * FIRST[s] : 3 * FIRST[s] + n].astype(F32).astype(BF)
        out[...] = dot(sel, wide, NT).astype(BF)


def assemble_weights(a):
    d = a.shape[1]
    return pl.pallas_call(
        assemble_kernel,
        out_shape=tuple(jax.ShapeDtypeStruct((3 * n, d), BF) for n in ROWS),
        in_specs=[VMEM],
        out_specs=(VMEM,) * 3,
        compiler_params=params(24),
    )(a)


def part_kernel(
    nrm, nrm_t, cot, cot_t, wx, wy, wz, after, gx, gy, gz, hid, w, back,
):
    total = nrm.shape[0]
    for s, src in enumerate((wx, wy, wz)):
        n = ROWS[s]
        for m in range(3):
            w[m * PART + FIRST[s] : m * PART + FIRST[s] + n, :] = src[m * n : (m + 1) * n, :]

    def body(i, _):
        at = pl.ds(pl.multiple_of(i * TB, TB), TB)
        gu = dot(w[: 2 * PART, :], nrm_t[:, at])
        dh = dot(w[2 * PART :, :], cot_t[:, at])
        g, u = gu[:PART], gu[PART:]
        s = 0.5 * jnp.tanh(0.5 * g) + 0.5
        silu = g * s
        h = (silu * u).astype(BF)
        back[:PART, at] = (dh * u * s * (1.0 + g * (1.0 - s))).astype(BF)
        back[PART : 2 * PART, at] = (dh * silu).astype(BF)
        back[2 * PART :, at] = h
        hid[:, at] = h
        return 0

    lax.fori_loop(0, total // TB, body, 0)
    w[: 2 * PART, :] = dot(back[: 2 * PART, :], nrm[...]).astype(BF)
    w[2 * PART :, :] = dot(back[2 * PART :, :], cot[...]).astype(BF)
    for s, dst in enumerate((gx, gy, gz)):
        n = ROWS[s]
        for m in range(3):
            dst[m * n : (m + 1) * n, :] = w[m * PART + FIRST[s] : m * PART + FIRST[s] + n, :]


def one_part(nrm, nrm_t, cot, cot_t, weights, after):
    total, d = nrm.shape
    out = pl.pallas_call(
        part_kernel,
        out_shape=tuple(jax.ShapeDtypeStruct((3 * n, d), BF) for n in ROWS)
        + (jax.ShapeDtypeStruct((PART, total), BF),),
        in_specs=[VMEM] * 7 + [ANY],
        out_specs=(VMEM,) * 4,
        scratch_shapes=[pltpu.VMEM((3 * PART, d), BF), pltpu.VMEM((3 * PART, total), BF)],
        compiler_params=params(28),
        cost_estimate=pl.CostEstimate(
            flops=6_000_000_000, bytes_accessed=16_000_000, transcendentals=500_000
        ),
    )(nrm, nrm_t, cot, cot_t, *weights, after)
    return out[:3], out[3]


def mix_kernel(tok_ref, *refs):
    hids, weights, (own_ref, far_ref), (hid, wd, tok, sems) = (
        refs[:4], refs[4:16], refs[16:18], refs[18:],
    )
    rows = own_ref.shape[0]
    copies = [(tok_ref.at[0], tok)]
    for k in range(4):
        copies.append((hids[k], hid.at[k * PART : (k + 1) * PART]))
        for s in range(3):
            n, at = ROWS[s], k * PART + FIRST[s]
            copies.append((weights[3 * k + s].at[2 * n : 3 * n], wd.at[at : at + n]))
    copies = [pltpu.make_async_copy(a, b, sems.at[i]) for i, (a, b) in enumerate(copies)]
    for copy in copies:
        copy.start()
    for copy in copies:
        copy.wait()
    for i in range(2 * rows // TB):
        at = slice(i * TB, (i + 1) * TB)
        total = dot(hid[:, at].T, wd[...])
        if i * TB < rows:
            own_ref[at, :] = total + tok[at, :].astype(F32)
        else:
            far_ref[i * TB - rows : (i + 1) * TB - rows, :] = total.astype(BF)


def mix(tok, hids, weights):
    _, rows, d = tok.shape
    return pl.pallas_call(
        mix_kernel,
        out_shape=(jax.ShapeDtypeStruct((rows, d), F32), jax.ShapeDtypeStruct((rows, d), BF)),
        in_specs=[ANY] * 17,
        out_specs=(VMEM,) * 2,
        scratch_shapes=[
            pltpu.VMEM((4 * PART, 2 * rows), BF),
            pltpu.VMEM((4 * PART, d), BF),
            pltpu.VMEM((rows, d), BF),
            pltpu.SemaphoreType.DMA((17,)),
        ],
        compiler_params=params(60),
        cost_estimate=pl.CostEstimate(
            flops=3_500_000_000, bytes_accessed=16_000_000, transcendentals=0
        ),
    )(tok, *hids, *[w for part in weights for w in part])


def pack_grads_kernel(*refs):
    out_ref, rows_ref = refs[12], refs[13]
    d = out_ref.shape[1]
    for s in range(3):
        total = refs[s][...].astype(F32)
        for k in range(1, 4):
            total = total + refs[3 * k + s][...].astype(F32)
        rows_ref[3 * FIRST[s] : 3 * FIRST[s] + 3 * ROWS[s], :] = total.astype(BF)
    rows_ref[3 * PART :, :] = jnp.zeros((1024 - 3 * PART, d), BF)
    turned = rows_ref[...].T
    for b in range(8):
        sel = assemble((1024, 1024), 0)[:, b * 128 : (b + 1) * 128].astype(F32).astype(BF)
        out_ref[b] = dot(turned, sel).astype(BF)


def pack_grads(parts):
    d = parts[0][0].shape[1]
    return pl.pallas_call(
        pack_grads_kernel,
        out_shape=jax.ShapeDtypeStruct((8, d, 128), BF),
        in_specs=[VMEM] * 12,
        out_specs=VMEM,
        scratch_shapes=[pltpu.VMEM((1024, d), BF)],
        compiler_params=params(40),
    )(*[g for part in parts for g in part])


def update_kernel(a_ref, *refs):
    (proj, proj_m, proj_v, down, down_m, down_v), outs = refs[:6], refs[6:]
    h, d = down.shape
    sums = [[None] * 4 for _ in range(3)]
    for x in range(4):
        for zl in range(2):
            for y in range(4):
                for zh in range(2):
                    v = a_ref[((x * 2 + zl) * 4 + y) * 2 + zh].astype(F32)
                    for s, p in enumerate((x, y, zh * 2 + zl)):
                        sums[s][p] = v if sums[s][p] is None else sums[s][p] + v
    wide = jnp.concatenate([v for part in sums for v in part], axis=1)
    high = wide.astype(BF)
    low = (wide - high.astype(F32)).astype(BF)
    for k in range(3):
        sel = place(k, (h, 1536), 0).astype(BF)
        grad = dot(sel, high, NT) + dot(sel, low, NT)
        if k < 2:
            new = adam(proj[k], grad, proj_m[k], proj_v[k])
            for out, v in zip(outs[:3], new):
                out[k] = v
        else:
            new = adam(down[...], grad, down_m[...], down_v[...])
            for out, v in zip(outs[3:], new):
                out[...] = v


def update(pieces, proj, proj_m, proj_v, down, down_m, down_v):
    shape = lambda a: jax.ShapeDtypeStruct(a.shape, F32)
    return pl.pallas_call(
        update_kernel,
        out_shape=(shape(proj),) * 3 + (shape(down),) * 3,
        in_specs=[VMEM] * 7,
        out_specs=(VMEM,) * 6,
        compiler_params=params(24),
    )(pieces, proj, proj_m, proj_v, down, down_m, down_v)


def shift_pairs(sizes, axis, hops):
    pairs = []
    nx, nzl, nc, ny, nzh = sizes
    line = lambda x, zl, c, y, zh: (((x * nzl + zl) * nc + c) * ny + y) * nzh + zh
    for x in range(nx):
        for zl in range(nzl):
            for c in range(nc):
                for y in range(ny):
                    for zh in range(nzh):
                        to = [x, y, zh * nzl + zl]
                        to[axis] = (to[axis] + hops) % (nx, ny, nzh * nzl)[axis]
                        pairs.append(
                            (
                                line(x, zl, c, y, zh),
                                line(to[0], to[2] % nzl, c, to[1], to[2] // nzl),
                            )
                        )
    return pairs


def shifted(parts, hops):
    sizes = tuple(lax.axis_size(a) for a in AXES)
    return tuple(
        lax.ppermute(v, AXES, shift_pairs(sizes, axis, hops)) for axis, v in enumerate(parts)
    )


def swap_cores(v):
    return lax.ppermute(v, "c", [(0, 1), (1, 0)])


def per_device(
    x_in, cotangent, seq_len, seq_owner, proj_master, down_master, proj_m, proj_v, down_m, down_v
):
    rows, d = cotangent.shape
    me = (lax.axis_index("y") * lax.axis_size("zh") + lax.axis_index("zh")).reshape(1)
    counts, owners = seq_len[0], seq_owner[0]
    flip = lambda v: jnp.swapaxes(v, 1, 2)
    slots, packed = pack(me, counts, owners, x_in, flip(proj_master), down_master)
    slots = lax.all_to_all(slots, ("y", "zh"), 0, 0, tiled=True)
    packed, slots = lax.optimization_barrier((packed, slots))
    arrived = lax.all_to_all(packed, GROUP, 0, 0, tiled=True)
    near_in = unpack(me, counts, owners, slots, cotangent, arrived)
    acts = turn(near_in, swap_cores(near_in))
    own = assemble_weights(arrived.reshape(8, d, 128))
    weights = [shifted(own, -k) for k in HOPS] + [own]
    grads, hids, after = [], [], near_in
    for w in weights:
        g, after = one_part(*acts, w, after)
        grads.append(g)
        hids.append(after)
    sums = [shifted(g, k) for g, k in zip(grads, HOPS)] + [grads[3]]
    messages = pack_grads(sums).reshape(64, d // 8, 128)
    pieces = lax.all_to_all(messages, GROUP, 0, 0, tiled=True)
    near, far = mix(near_in, hids, weights)
    mixed = (near + swap_cores(far).astype(F32)).astype(BF)
    out = update(
        pieces, flip(proj_master), flip(proj_m), flip(proj_v), down_master, down_m, down_v
    )
    new_proj, new_proj_m, new_proj_v = (flip(v) for v in out[:3])
    new_down, new_down_m, new_down_v = out[3:]
    return (mixed, new_proj, new_down, new_proj_m, new_proj_v, new_down_m, new_down_v)


def solution(mesh):
    mesh = Mesh(mesh.devices.reshape(4, 2, 2, 4, 2), AXES)
    blk, dp = ("x", "zl", "c"), ("y", "zh")
    in_specs = (
        P(blk + dp, None),
        P(blk + dp, None),
        P(blk, None, None),
        P(blk, None, None),
        P(None, dp, blk),
        P(blk, dp),
        P(None, dp, blk),
        P(None, dp, blk),
        P(blk, dp),
        P(blk, dp),
    )
    out_specs = (
        P(blk + dp, None),
        P(None, dp, blk),
        P(blk, dp),
        P(None, dp, blk),
        P(None, dp, blk),
        P(blk, dp),
        P(blk, dp),
    )
    return jax.shard_map(
        per_device, mesh=mesh, in_specs=in_specs, out_specs=out_specs, check_vma=False
    )
```

```python
import jax
import jax.numpy as jnp
import numpy as np
from jax import lax
from jax.experimental import pallas as pl
from jax.experimental.pallas import tpu as pltpu
from jax.sharding import Mesh, PartitionSpec as P

STEP = 100
AXES = ("x", "zl", "c", "y", "zh")
GROUP = ("x", "zl", "y", "zh")
BF = jnp.bfloat16
F32 = jnp.float32
SLOT = 208
WIN = 256
NT = (((1,), (1,)), ((), ()))
MB = 1024 * 1024
SIZE = (26, 12)
LANE = (0, 78)
UNIT = (0, 104)
UNITS = 152
ROWS = tuple(8 * n for n in SIZE)
PART = sum(ROWS)
FIRST = (0, ROWS[0])
STREAMS = len(SIZE)
COLS = STREAMS * 512
HOPS = (2, -1, 1)


def dot(a, b, dims=(((1,), (0,)), ((), ()))):
    return lax.dot_general(a, b, dims, preferred_element_type=F32)


def iota(shape, dim):
    return lax.broadcasted_iota(jnp.int32, shape, dim)


def adam(master, grad, first_moment, second_moment):
    first_new = 0.9 * first_moment + 0.1 * grad
    second_new = 0.95 * second_moment + 0.05 * grad * grad
    first_hat = first_new / (1.0 - 0.9**STEP)
    second_hat = second_new / (1.0 - 0.95**STEP)
    updated = master - 0.0003 * (first_hat / (jnp.sqrt(second_hat) + 1e-08) + 0.1 * master)
    return (updated, first_new, second_new)


VMEM = pl.BlockSpec(memory_space=pltpu.VMEM)
SMEM = pl.BlockSpec(memory_space=pltpu.SMEM)
ANY = pl.BlockSpec(memory_space=pl.ANY)
TB = 256


def params(size):
    return pltpu.CompilerParams(vmem_limit_bytes=size * MB)


def by_stream(index, values):
    out = jnp.full(index.shape, values[0], jnp.int32)
    for s in range(1, STREAMS):
        out = jnp.where(index == s, values[s], out)
    return out


def place(matrix):
    col = iota((1, COLS), 1)
    stream, part, lane = col // 512, (col // 128) % 4, col % 128
    size = by_stream(stream, SIZE)
    i = lane - by_stream(stream, LANE) - matrix * size
    target = jnp.where((i >= 0) & (i < size), by_stream(stream, UNIT) + size * part + i, -1)
    return (iota((UNITS, COLS), 0) == target).astype(F32).astype(BF)


def assembling():
    out = np.zeros((1024, 1024), np.float32)
    for s, size in enumerate(SIZE):
        for m in range(3):
            for b in range(8):
                for i in range(size):
                    row = 3 * FIRST[s] + m * 8 * size + b * size + i
                    out[row, b * 128 + LANE[s] + m * size + i] = 1
    return jnp.asarray(out, BF)


def others():
    return [
        (((x * 2 + zl) * 4 + y) * 2 + zh, x, y, zh * 2 + zl)
        for x in range(4)
        for zl in range(2)
        for y in range(4)
        for zh in range(2)
    ]


def pack_kernel(
    me_ref, core_ref, len_ref, own_ref, x_ref, proj_ref, down_ref, slots_ref, out_ref,
    rows_ref, proj, down, slots, lens, owns, starts, sems, out_sems,
):
    pairs = (
        (proj_ref, proj), (down_ref, down), (len_ref, lens), (own_ref, owns), (x_ref, rows_ref),
    )
    copies = [pltpu.make_async_copy(a, b, sems.at[k]) for k, (a, b) in enumerate(pairs)]
    for copy in copies:
        copy.start()
    d = down.shape[1]
    eye = (iota((d, d), 0) == iota((d, d), 1)).astype(BF)
    total = jnp.zeros((d, COLS), F32)
    for copy in copies[:2]:
        copy.wait()
    for k in range(3):
        m = (down[...] if k == 2 else proj[k]).astype(BF)
        turned = dot(eye, m, NT).astype(BF)
        total = total + dot(turned, place(k))
    total = total.astype(BF)
    at = lambda s, p: total[:, s * 512 + p * 128 : s * 512 + (p + 1) * 128]
    for core in range(2):

        @pl.when(core_ref[0] == core)
        def _():
            for index, x, y, z in others():
                out_ref[index] = at(0, z if core else x) + at(1, y)

    copies[2].wait()
    copies[3].wait()
    n = lens.shape[1]
    rows = rows_ref.shape[0]
    me = me_ref[0]
    first = jnp.int32(0)
    for k in range(n):
        starts[owns[me, k]] = first
        first = first + lens[me, k]
    copies[4].wait()
    sent = []
    for g in range(n):
        begin = starts[g]
        base = pl.multiple_of(jnp.minimum((begin // 16) * 16, rows - WIN), 16)
        hot = (iota((SLOT, WIN), 1) - iota((SLOT, WIN), 0) == begin - base).astype(BF)
        slots[g] = dot(hot, rows_ref[pl.ds(base, WIN), :]).astype(BF)
        sent.append(pltpu.make_async_copy(slots.at[g], slots_ref.at[g], out_sems.at[g]))
        sent[-1].start()
    for copy in sent:
        copy.wait()


def pack(me, core, seq_len, seq_owner, x_in, proj, down):
    n = seq_len.shape[0]
    slots = (n, SLOT, x_in.shape[1])
    return pl.pallas_call(
        pack_kernel,
        out_shape=(
            jax.ShapeDtypeStruct(slots, BF),
            jax.ShapeDtypeStruct((64, down.shape[1], 128), BF),
        ),
        in_specs=[SMEM] * 2 + [ANY] * 5,
        out_specs=(ANY, VMEM),
        scratch_shapes=[
            pltpu.VMEM(x_in.shape, BF),
            pltpu.VMEM(proj.shape, F32),
            pltpu.VMEM(down.shape, F32),
            pltpu.VMEM(slots, BF),
            pltpu.SMEM((n, n), jnp.int32),
            pltpu.SMEM((n, n), jnp.int32),
            pltpu.SMEM((n,), jnp.int32),
            pltpu.SemaphoreType.DMA((5,)),
            pltpu.SemaphoreType.DMA((n,)),
        ],
        compiler_params=params(58),
    )(me, core, seq_len, seq_owner, x_in, proj, down)


def unpack_kernel(me_ref, len_ref, own_ref, slots_ref, cot_ref, after_ref, out_ref, acc_ref):
    n = len_ref.shape[0]
    rows = out_ref.shape[1]
    me = me_ref[0]
    acc_ref[...] = jnp.zeros_like(acc_ref)
    at = jnp.int32(0)
    for g in range(n):
        count = jnp.int32(0)
        for k in range(n):
            count = count + jnp.where(own_ref[g, k] == me, len_ref[g, k], 0)
        base = pl.multiple_of((at // 16) * 16, 16)
        row, col = iota((WIN, SLOT), 0), iota((WIN, SLOT), 1)
        sel = ((row - col == at - base) & (col < count)).astype(BF)
        acc_ref[pl.ds(base, WIN), :] += dot(sel, slots_ref[g]).astype(BF)
        at = at + count
    out_ref[0] = acc_ref[:rows, :]
    out_ref[1] = cot_ref[...]


def unpack(me, seq_len, seq_owner, slots, cot, after):
    rows, d = cot.shape
    return pl.pallas_call(
        unpack_kernel,
        out_shape=jax.ShapeDtypeStruct((2, rows, d), BF),
        in_specs=[SMEM, SMEM, SMEM, VMEM, VMEM, ANY],
        out_specs=VMEM,
        scratch_shapes=[pltpu.VMEM((rows + WIN, d), BF)],
        compiler_params=params(24),
    )(me, seq_len, seq_owner, slots, cot, after)


def turn_kernel(a_ref, b_ref, nrm_ref, nrm_t_ref, cot_ref, cot_t_ref):
    rows = a_ref.shape[1]
    for half, ref in enumerate((a_ref, b_ref)):
        for i in range(rows // TB):
            at = half * rows + i * TB
            t = ref[0, i * TB : (i + 1) * TB, :].astype(F32)
            scale = lax.rsqrt(jnp.mean(t * t, axis=1, keepdims=True) + 1e-06)
            t = (t * scale).astype(BF)
            nrm_ref[at : at + TB, :] = t
            nrm_t_ref[:, at : at + TB] = t.T
            c = ref[1, i * TB : (i + 1) * TB, :]
            cot_ref[at : at + TB, :] = c
            cot_t_ref[:, at : at + TB] = c.T


def turn(a, b):
    _, rows, d = a.shape
    flat, turned = jax.ShapeDtypeStruct((2 * rows, d), BF), jax.ShapeDtypeStruct((d, 2 * rows), BF)
    return pl.pallas_call(
        turn_kernel,
        out_shape=(flat, turned, flat, turned),
        in_specs=[VMEM] * 2,
        out_specs=(VMEM,) * 4,
        compiler_params=params(30),
    )(a, b)


def assemble_kernel(a_ref, sel_ref, *out_refs):
    wide = jnp.concatenate([a_ref[b] for b in range(8)], axis=1)
    for s, out in enumerate(out_refs):
        at = slice(3 * FIRST[s], 3 * FIRST[s] + 3 * ROWS[s])
        out[...] = dot(sel_ref[at, :], wide, NT).astype(BF)


def assemble_weights(a, sel):
    d = a.shape[1]
    return pl.pallas_call(
        assemble_kernel,
        out_shape=tuple(jax.ShapeDtypeStruct((3 * n, d), BF) for n in ROWS),
        in_specs=[VMEM] * 2,
        out_specs=(VMEM,) * STREAMS,
        compiler_params=params(24),
    )(a, sel)


def part_kernel(
    nrm, nrm_t, cot, cot_t, wx, wy, *refs,
):
    gx, gy, hid, w, back = refs[-5:]
    total = nrm.shape[0]
    for s, src in enumerate((wx, wy)):
        n = ROWS[s]
        for m in range(3):
            w[m * PART + FIRST[s] : m * PART + FIRST[s] + n, :] = src[m * n : (m + 1) * n, :]

    def body(i, _):
        at = pl.ds(pl.multiple_of(i * TB, TB), TB)
        gu = dot(w[: 2 * PART, :], nrm_t[:, at])
        dh = dot(w[2 * PART :, :], cot_t[:, at])
        g, u = gu[:PART], gu[PART:]
        s = 0.5 * jnp.tanh(0.5 * g) + 0.5
        silu = g * s
        h = (silu * u).astype(BF)
        back[:PART, at] = (dh * u * s * (1.0 + g * (1.0 - s))).astype(BF)
        back[PART : 2 * PART, at] = (dh * silu).astype(BF)
        back[2 * PART :, at] = h
        hid[:, at] = h
        return 0

    lax.fori_loop(0, total // TB, body, 0, unroll=True)
    w[: 2 * PART, :] = dot(back[: 2 * PART, :], nrm[...]).astype(BF)
    w[2 * PART :, :] = dot(back[2 * PART :, :], cot[...]).astype(BF)
    for s, dst in enumerate((gx, gy)):
        n = ROWS[s]
        for m in range(3):
            dst[m * n : (m + 1) * n, :] = w[m * PART + FIRST[s] : m * PART + FIRST[s] + n, :]


def one_part(nrm, nrm_t, cot, cot_t, weights, after):
    total, d = nrm.shape
    out = pl.pallas_call(
        part_kernel,
        out_shape=tuple(jax.ShapeDtypeStruct((3 * n, d), BF) for n in ROWS)
        + (jax.ShapeDtypeStruct((PART, total), BF),),
        in_specs=[VMEM] * (4 + STREAMS) + [ANY] * len(after),
        out_specs=(VMEM,) * (STREAMS + 1),
        scratch_shapes=[pltpu.VMEM((3 * PART, d), BF), pltpu.VMEM((3 * PART, total), BF)],
        compiler_params=params(28),
        cost_estimate=pl.CostEstimate(
            flops=200_000_000, bytes_accessed=400_000, transcendentals=10_000
        ),
    )(nrm, nrm_t, cot, cot_t, *weights, *after)
    return out[:STREAMS], out[STREAMS]


def mix_kernel(tok_ref, *refs):
    hids, weights, (own_ref, far_ref), (hid, wd, tok, sems) = (
        refs[:4], refs[4:12], refs[12:14], refs[14:],
    )
    rows = own_ref.shape[0]
    copies = [(tok_ref.at[0], tok)]
    for k in range(4):
        copies.append((hids[k], hid.at[k * PART : (k + 1) * PART]))
        for s in range(STREAMS):
            n, at = ROWS[s], k * PART + FIRST[s]
            copies.append((weights[STREAMS * k + s].at[2 * n : 3 * n], wd.at[at : at + n]))
    copies = [pltpu.make_async_copy(a, b, sems.at[i]) for i, (a, b) in enumerate(copies)]
    for copy in copies:
        copy.start()
    for copy in copies:
        copy.wait()
    for i in range(2 * rows // TB):
        at = slice(i * TB, (i + 1) * TB)
        total = dot(hid[:, at].T, wd[...])
        if i * TB < rows:
            own_ref[at, :] = total + tok[at, :].astype(F32)
        else:
            far_ref[i * TB - rows : (i + 1) * TB - rows, :] = total.astype(BF)


def mix(tok, hids, weights):
    _, rows, d = tok.shape
    return pl.pallas_call(
        mix_kernel,
        out_shape=(jax.ShapeDtypeStruct((rows, d), F32), jax.ShapeDtypeStruct((rows, d), BF)),
        in_specs=[ANY] * 13,
        out_specs=(VMEM,) * 2,
        scratch_shapes=[
            pltpu.VMEM((4 * PART, 2 * rows), BF),
            pltpu.VMEM((4 * PART, d), BF),
            pltpu.VMEM((rows, d), BF),
            pltpu.SemaphoreType.DMA((13,)),
        ],
        compiler_params=params(60),
        cost_estimate=pl.CostEstimate(
            flops=3_500_000_000, bytes_accessed=16_000_000, transcendentals=0
        ),
    )(tok, *hids, *[w for part in weights for w in part])


def pack_grads_kernel(*refs):
    sel_ref, out_ref, rows_ref = refs[4 * STREAMS :]
    d = out_ref.shape[1]
    for s in range(STREAMS):
        total = refs[s][...].astype(F32)
        for k in range(1, 4):
            total = total + refs[STREAMS * k + s][...].astype(F32)
        rows_ref[3 * FIRST[s] : 3 * FIRST[s] + 3 * ROWS[s], :] = total.astype(BF)
    rows_ref[3 * PART :, :] = jnp.zeros((1024 - 3 * PART, d), BF)
    turned = rows_ref[...].T
    for b in range(0, 8, 2):
        pair = dot(turned, sel_ref[:, b * 128 : (b + 2) * 128]).astype(BF)
        for k in range(2):
            out_ref[b + k] = pair[:, k * 128 : (k + 1) * 128]


def pack_grads(parts, sel):
    d = parts[0][0].shape[1]
    return pl.pallas_call(
        pack_grads_kernel,
        out_shape=jax.ShapeDtypeStruct((8, d, 128), BF),
        in_specs=[VMEM] * (4 * STREAMS + 1),
        out_specs=VMEM,
        scratch_shapes=[pltpu.VMEM((1024, d), BF)],
        compiler_params=params(40),
    )(*[g for part in parts for g in part], sel)


def update_kernel(core_ref, a_ref, *refs):
    (proj, proj_m, proj_v, down, down_m, down_v), outs, (wide_ref,) = (
        refs[:6], refs[6:12], refs[12:],
    )
    for core in range(2):

        @pl.when(core_ref[0] == core)
        def _():
            sums = [[None] * 4 for _ in range(STREAMS)]
            for index, x, y, z in others():
                v = a_ref[index].astype(F32)
                for s, p in enumerate((z if core else x, y)):
                    sums[s][p] = v if sums[s][p] is None else sums[s][p] + v
            wide_ref[...] = jnp.concatenate([v for part in sums for v in part], axis=1)

    wide = wide_ref[...]
    high = wide.astype(BF)
    low = (wide - high.astype(F32)).astype(BF)
    for k in range(3):
        sel = place(k)
        grad = dot(sel, high, NT) + dot(sel, low, NT)
        if k < 2:
            new = adam(proj[k], grad, proj_m[k], proj_v[k])
            for out, v in zip(outs[:3], new):
                out[k] = v
        else:
            new = adam(down[...], grad, down_m[...], down_v[...])
            for out, v in zip(outs[3:], new):
                out[...] = v


def update(core, pieces, proj, proj_m, proj_v, down, down_m, down_v):
    shape = lambda a: jax.ShapeDtypeStruct(a.shape, F32)
    return pl.pallas_call(
        update_kernel,
        out_shape=(shape(proj),) * 3 + (shape(down),) * 3,
        in_specs=[SMEM] + [VMEM] * 7,
        out_specs=(VMEM,) * 6,
        scratch_shapes=[pltpu.VMEM((down.shape[1], COLS), F32)],
        compiler_params=params(24),
    )(core, pieces, proj, proj_m, proj_v, down, down_m, down_v)


def shift_pairs(sizes, stream, hops):
    pairs = []
    nx, nzl, nc, ny, nzh = sizes
    line = lambda x, zl, c, y, zh: (((x * nzl + zl) * nc + c) * ny + y) * nzh + zh
    for x in range(nx):
        for zl in range(nzl):
            for c in range(nc):
                for y in range(ny):
                    for zh in range(nzh):
                        to = [x, y, zh * nzl + zl]
                        axis = 1 if stream else (0, 2)[c]
                        step = -hops if c else hops
                        to[axis] = (to[axis] + step) % (nx, ny, nzh * nzl)[axis]
                        pairs.append(
                            (
                                line(x, zl, c, y, zh),
                                line(to[0], to[2] % nzl, c, to[1], to[2] // nzl),
                            )
                        )
    return pairs


def shifted(parts, hops):
    sizes = tuple(lax.axis_size(a) for a in AXES)
    return tuple(
        lax.ppermute(v, AXES, shift_pairs(sizes, stream, hops)) for stream, v in enumerate(parts)
    )


def swap_cores(v):
    return lax.ppermute(v, "c", [(0, 1), (1, 0)])


def per_device(
    x_in, cotangent, seq_len, seq_owner, proj_master, down_master, proj_m, proj_v, down_m, down_v
):
    rows, d = cotangent.shape
    me = (lax.axis_index("y") * lax.axis_size("zh") + lax.axis_index("zh")).reshape(1)
    core = lax.axis_index("c").reshape(1)
    counts, owners = seq_len[0], seq_owner[0]
    flip = lambda v: jnp.swapaxes(v, 1, 2)
    rows_of = assembling()
    slots, packed = pack(me, core, counts, owners, x_in, flip(proj_master), down_master)
    slots = lax.all_to_all(slots, ("y", "zh"), 0, 0, tiled=True)
    packed, slots = lax.optimization_barrier((packed, slots))
    arrived = lax.all_to_all(packed, GROUP, 0, 0, tiled=True)
    own = assemble_weights(arrived.reshape(8, d, 128), rows_of)
    near_in = unpack(me, counts, owners, slots, cotangent, own[0])
    acts = turn(near_in, swap_cores(near_in))
    weights = [shifted(own, -k) for k in HOPS] + [own]
    sums, hids, after = [], [], [near_in]
    for i, w in enumerate(weights):
        if i == 2:
            after += sums[0][1:]
        g, h = one_part(*acts, w, after)
        sums.append(shifted(g, HOPS[i]) if i < 3 else g)
        hids.append(h)
        after = [h]
    messages = pack_grads(sums, rows_of).reshape(64, d // 8, 128)
    pieces = lax.all_to_all(messages, GROUP, 0, 0, tiled=True)
    near, far = mix(near_in, hids, weights)
    mixed = (near + swap_cores(far).astype(F32)).astype(BF)
    out = update(
        core, pieces, flip(proj_master), flip(proj_m), flip(proj_v), down_master, down_m, down_v
    )
    new_proj, new_proj_m, new_proj_v = (flip(v) for v in out[:3])
    new_down, new_down_m, new_down_v = out[3:]
    return (mixed, new_proj, new_down, new_proj_m, new_proj_v, new_down_m, new_down_v)


def solution(mesh):
    mesh = Mesh(mesh.devices.reshape(4, 2, 2, 4, 2), AXES)
    blk, dp = ("x", "zl", "c"), ("y", "zh")
    in_specs = (
        P(blk + dp, None),
        P(blk + dp, None),
        P(blk, None, None),
        P(blk, None, None),
        P(None, dp, blk),
        P(blk, dp),
        P(None, dp, blk),
        P(None, dp, blk),
        P(blk, dp),
        P(blk, dp),
    )
    out_specs = (
        P(blk + dp, None),
        P(None, dp, blk),
        P(blk, dp),
        P(None, dp, blk),
        P(None, dp, blk),
        P(blk, dp),
        P(blk, dp),
    )
    return jax.shard_map(
        per_device, mesh=mesh, in_specs=in_specs, out_specs=out_specs, check_vma=False
    )
```

```python
import jax
import jax.numpy as jnp
from jax import lax
from jax.experimental import pallas as pl
from jax.experimental.pallas import tpu as pltpu
from jax.sharding import Mesh, PartitionSpec as P

STEP = 100
AXES = ("x", "zl", "c", "y", "zh")
GROUP = ("x", "zl", "y", "zh")
BF = jnp.bfloat16
F32 = jnp.float32
SLOT = 208
WIN = 256
NT = (((1,), (1,)), ((), ()))
MB = 1024 * 1024
SIZE = (26, 12)
LANE = (0, 78)
UNIT = (0, 104)
UNITS = 152
ROWS = tuple(8 * n for n in SIZE)
PART = sum(ROWS)
FIRST = (0, ROWS[0])
STREAMS = len(SIZE)
COLS = STREAMS * 512
HOPS = (2, -1, 1)


def dot(a, b, dims=(((1,), (0,)), ((), ()))):
    return lax.dot_general(a, b, dims, preferred_element_type=F32)


def iota(shape, dim):
    return lax.broadcasted_iota(jnp.int32, shape, dim)


def adam(master, grad, first_moment, second_moment):
    first_new = 0.9 * first_moment + 0.1 * grad
    second_new = 0.95 * second_moment + 0.05 * grad * grad
    first_hat = first_new / (1.0 - 0.9**STEP)
    second_hat = second_new / (1.0 - 0.95**STEP)
    updated = master - 0.0003 * (first_hat / (jnp.sqrt(second_hat) + 1e-08) + 0.1 * master)
    return (updated, first_new, second_new)


VMEM = pl.BlockSpec(memory_space=pltpu.VMEM)
SMEM = pl.BlockSpec(memory_space=pltpu.SMEM)
ANY = pl.BlockSpec(memory_space=pl.ANY)
TB = 256


def params(size):
    return pltpu.CompilerParams(vmem_limit_bytes=size * MB)


def by_stream(index, values):
    out = jnp.full(index.shape, values[0], jnp.int32)
    for s in range(1, STREAMS):
        out = jnp.where(index == s, values[s], out)
    return out


def place(matrix):
    col = iota((1, COLS), 1)
    stream, part, lane = col // 512, (col // 128) % 4, col % 128
    size = by_stream(stream, SIZE)
    i = lane - by_stream(stream, LANE) - matrix * size
    target = jnp.where((i >= 0) & (i < size), by_stream(stream, UNIT) + size * part + i, -1)
    return (iota((UNITS, COLS), 0) == target).astype(F32).astype(BF)


def assemble(stream):
    size, rows = SIZE[stream], 3 * ROWS[stream]
    row = iota((rows, 1), 0)
    matrix = (row >= 8 * size).astype(jnp.int32) + (row >= 16 * size).astype(jnp.int32)
    out = []
    for block in range(8):
        i = row - matrix * 8 * size - block * size
        target = jnp.where((i >= 0) & (i < size), LANE[stream] + matrix * size + i, -1)
        out.append((iota((rows, 128), 1) == target).astype(F32).astype(BF))
    return jnp.concatenate(out, axis=1)


def others():
    return [
        (((x * 2 + zl) * 4 + y) * 2 + zh, x, y, zh * 2 + zl)
        for x in range(4)
        for zl in range(2)
        for y in range(4)
        for zh in range(2)
    ]


def pack_kernel(
    me_ref, core_ref, len_ref, own_ref, x_ref, proj_ref, down_ref, slots_ref, out_ref,
    rows_ref, proj, down, parts, slots, lens, owns, starts, sems, out_sems,
):
    pairs = (
        (proj_ref, proj), (down_ref, down), (len_ref, lens), (own_ref, owns), (x_ref, rows_ref),
    )
    copies = [pltpu.make_async_copy(a, b, sems.at[k]) for k, (a, b) in enumerate(pairs)]
    for copy in copies:
        copy.start()
    d = down.shape[1]
    eye = (iota((d, d), 0) == iota((d, d), 1)).astype(BF)
    total = jnp.zeros((d, COLS), F32)
    for copy in copies[:2]:
        copy.wait()
    for k in range(3):
        m = (down[...] if k == 2 else proj[k]).astype(BF)
        turned = dot(eye, m, NT).astype(BF)
        total = total + dot(turned, place(k))
    total = total.astype(BF)
    for k in range(4 * STREAMS):
        parts[k] = total[:, k * 128 : (k + 1) * 128]
    core = core_ref[0]

    def messages(x, _):
        for k in range(16):
            zl, y, zh = k // 8, (k // 2) % 4, k % 2
            along = jnp.where(core == 0, x, zh * 2 + zl)
            out_ref[x * 16 + k] = parts[along] + parts[4 + y]
        return 0

    lax.fori_loop(0, 4, messages, 0)
    copies[2].wait()
    copies[3].wait()
    n = lens.shape[1]
    rows = rows_ref.shape[0]
    me = me_ref[0]
    first = jnp.int32(0)
    for k in range(n):
        starts[owns[me, k]] = first
        first = first + lens[me, k]
    copies[4].wait()

    def send(g):
        return pltpu.make_async_copy(slots.at[g], slots_ref.at[g], out_sems.at[g])

    def fill(g, _):
        begin = starts[g]
        base = pl.multiple_of(jnp.minimum((begin // 16) * 16, rows - WIN), 16)
        hot = (iota((SLOT, WIN), 1) - iota((SLOT, WIN), 0) == begin - base).astype(BF)
        slots[g] = dot(hot, rows_ref[pl.ds(base, WIN), :]).astype(BF)
        send(g).start()
        return 0

    for g in range(n):
        fill(g, 0)
    for g in range(n):
        send(g).wait()


def pack(me, core, seq_len, seq_owner, x_in, proj, down):
    n = seq_len.shape[0]
    slots = (n, SLOT, x_in.shape[1])
    return pl.pallas_call(
        pack_kernel,
        out_shape=(
            jax.ShapeDtypeStruct(slots, BF),
            jax.ShapeDtypeStruct((64, down.shape[1], 128), BF),
        ),
        in_specs=[SMEM] * 2 + [ANY] * 5,
        out_specs=(ANY, VMEM),
        scratch_shapes=[
            pltpu.VMEM(x_in.shape, BF),
            pltpu.VMEM(proj.shape, F32),
            pltpu.VMEM(down.shape, F32),
            pltpu.VMEM((4 * STREAMS, down.shape[1], 128), BF),
            pltpu.VMEM(slots, BF),
            pltpu.SMEM((n, n), jnp.int32),
            pltpu.SMEM((n, n), jnp.int32),
            pltpu.SMEM((n,), jnp.int32),
            pltpu.SemaphoreType.DMA((5,)),
            pltpu.SemaphoreType.DMA((n,)),
        ],
        compiler_params=params(58),
    )(me, core, seq_len, seq_owner, x_in, proj, down)


def unpack_kernel(me_ref, len_ref, own_ref, slots_ref, cot_ref, after_ref, out_ref, acc_ref):
    n = len_ref.shape[0]
    rows = out_ref.shape[1]
    me = me_ref[0]
    acc_ref[...] = jnp.zeros_like(acc_ref)

    def place_rows(g, at):
        count = jnp.int32(0)
        for k in range(n):
            count = count + jnp.where(own_ref[g, k] == me, len_ref[g, k], 0)
        base = pl.multiple_of((at // 16) * 16, 16)
        row, col = iota((WIN, SLOT), 0), iota((WIN, SLOT), 1)
        sel = ((row - col == at - base) & (col < count)).astype(BF)
        acc_ref[pl.ds(base, WIN), :] += dot(sel, slots_ref[g]).astype(BF)
        return at + count

    at = jnp.int32(0)
    for g in range(n):
        at = place_rows(g, at)
    out_ref[0] = acc_ref[:rows, :]
    out_ref[1] = cot_ref[...]


def unpack(me, seq_len, seq_owner, slots, cot, after):
    rows, d = cot.shape
    return pl.pallas_call(
        unpack_kernel,
        out_shape=jax.ShapeDtypeStruct((2, rows, d), BF),
        in_specs=[SMEM, SMEM, SMEM, VMEM, VMEM, ANY],
        out_specs=VMEM,
        scratch_shapes=[pltpu.VMEM((rows + WIN, d), BF)],
        compiler_params=params(24),
    )(me, seq_len, seq_owner, slots, cot, after)


def turn_kernel(a_ref, b_ref, nrm_ref, nrm_t_ref, cot_ref, cot_t_ref, sel_ref):
    for s in range(STREAMS):
        sel_ref[3 * FIRST[s] : 3 * FIRST[s] + 3 * ROWS[s], :] = assemble(s)
    sel_ref[3 * PART :, :] = jnp.zeros((1024 - 3 * PART, 1024), BF)
    rows = a_ref.shape[1]
    for half, ref in enumerate((a_ref, b_ref)):

        def body(i, _):
            src = pl.ds(pl.multiple_of(i * TB, TB), TB)
            at = pl.ds(pl.multiple_of(half * rows + i * TB, TB), TB)
            t = ref[0, src, :].astype(F32)
            scale = lax.rsqrt(jnp.mean(t * t, axis=1, keepdims=True) + 1e-06)
            t = (t * scale).astype(BF)
            nrm_ref[at, :] = t
            nrm_t_ref[:, at] = t.T
            c = ref[1, src, :]
            cot_ref[at, :] = c
            cot_t_ref[:, at] = c.T
            return 0

        lax.fori_loop(0, rows // TB, body, 0)


def turn(a, b):
    _, rows, d = a.shape
    flat, turned = jax.ShapeDtypeStruct((2 * rows, d), BF), jax.ShapeDtypeStruct((d, 2 * rows), BF)
    return pl.pallas_call(
        turn_kernel,
        out_shape=(flat, turned, flat, turned, jax.ShapeDtypeStruct((1024, 1024), BF)),
        in_specs=[VMEM] * 2,
        out_specs=(VMEM,) * 5,
        compiler_params=params(30),
    )(a, b)


def assemble_kernel(a_ref, *out_refs):
    wide = jnp.concatenate([a_ref[b] for b in range(8)], axis=1)
    for s, out in enumerate(out_refs):
        out[...] = dot(assemble(s), wide, NT).astype(BF)


def assemble_weights(a):
    d = a.shape[1]
    return pl.pallas_call(
        assemble_kernel,
        out_shape=tuple(jax.ShapeDtypeStruct((3 * n, d), BF) for n in ROWS),
        in_specs=[VMEM],
        out_specs=(VMEM,) * STREAMS,
        compiler_params=params(24),
    )(a)


def part_kernel(
    nrm, nrm_t, cot, cot_t, wx, wy, *refs,
):
    gx, gy, hid, w, back = refs[-5:]
    total = nrm.shape[0]
    for s, src in enumerate((wx, wy)):
        n = ROWS[s]
        for m in range(3):
            w[m * PART + FIRST[s] : m * PART + FIRST[s] + n, :] = src[m * n : (m + 1) * n, :]

    def body(i, _):
        at = pl.ds(pl.multiple_of(i * TB, TB), TB)
        gu = dot(w[: 2 * PART, :], nrm_t[:, at])
        dh = dot(w[2 * PART :, :], cot_t[:, at])
        g, u = gu[:PART], gu[PART:]
        s = 0.5 * jnp.tanh(0.5 * g) + 0.5
        silu = g * s
        h = (silu * u).astype(BF)
        back[:PART, at] = (dh * u * s * (1.0 + g * (1.0 - s))).astype(BF)
        back[PART : 2 * PART, at] = (dh * silu).astype(BF)
        back[2 * PART :, at] = h
        hid[:, at] = h
        return 0

    lax.fori_loop(0, total // TB, body, 0, unroll=3)
    w[: 2 * PART, :] = dot(back[: 2 * PART, :], nrm[...]).astype(BF)
    w[2 * PART :, :] = dot(back[2 * PART :, :], cot[...]).astype(BF)
    for s, dst in enumerate((gx, gy)):
        n = ROWS[s]
        for m in range(3):
            dst[m * n : (m + 1) * n, :] = w[m * PART + FIRST[s] : m * PART + FIRST[s] + n, :]


def one_part(nrm, nrm_t, cot, cot_t, weights, after):
    total, d = nrm.shape
    out = pl.pallas_call(
        part_kernel,
        out_shape=tuple(jax.ShapeDtypeStruct((3 * n, d), BF) for n in ROWS)
        + (jax.ShapeDtypeStruct((PART, total), BF),),
        in_specs=[VMEM] * (4 + STREAMS) + [ANY] * len(after),
        out_specs=(VMEM,) * (STREAMS + 1),
        scratch_shapes=[pltpu.VMEM((3 * PART, d), BF), pltpu.VMEM((3 * PART, total), BF)],
        compiler_params=params(28),
        cost_estimate=pl.CostEstimate(
            flops=200_000_000, bytes_accessed=400_000, transcendentals=10_000
        ),
    )(nrm, nrm_t, cot, cot_t, *weights, *after)
    return out[:STREAMS], out[STREAMS]


def mix_kernel(tok_ref, *refs):
    hids, weights, (own_ref, far_ref), (hid, wd, tok, sems) = (
        refs[:4], refs[4:12], refs[12:14], refs[14:],
    )
    rows = own_ref.shape[0]
    copies = [(tok_ref.at[0], tok)]
    for k in range(4):
        copies.append((hids[k], hid.at[k * PART : (k + 1) * PART]))
        for s in range(STREAMS):
            n, at = ROWS[s], k * PART + FIRST[s]
            copies.append((weights[STREAMS * k + s].at[2 * n : 3 * n], wd.at[at : at + n]))
    copies = [pltpu.make_async_copy(a, b, sems.at[i]) for i, (a, b) in enumerate(copies)]
    for copy in copies:
        copy.start()
    for copy in copies:
        copy.wait()

    def body(i, _):
        near = pl.ds(pl.multiple_of(i * TB, TB), TB)
        far = pl.ds(pl.multiple_of(rows + i * TB, TB), TB)
        own_ref[near, :] = dot(hid[:, near].T, wd[...]) + tok[near, :].astype(F32)
        far_ref[near, :] = dot(hid[:, far].T, wd[...]).astype(BF)
        return 0

    lax.fori_loop(0, rows // TB, body, 0)


def mix(tok, hids, weights):
    _, rows, d = tok.shape
    return pl.pallas_call(
        mix_kernel,
        out_shape=(jax.ShapeDtypeStruct((rows, d), F32), jax.ShapeDtypeStruct((rows, d), BF)),
        in_specs=[ANY] * 13,
        out_specs=(VMEM,) * 2,
        scratch_shapes=[
            pltpu.VMEM((4 * PART, 2 * rows), BF),
            pltpu.VMEM((4 * PART, d), BF),
            pltpu.VMEM((rows, d), BF),
            pltpu.SemaphoreType.DMA((13,)),
        ],
        compiler_params=params(60),
        cost_estimate=pl.CostEstimate(
            flops=3_500_000_000, bytes_accessed=16_000_000, transcendentals=0
        ),
    )(tok, *hids, *[w for part in weights for w in part])


def pack_grads_kernel(*refs):
    sel_ref, out_ref, rows_ref = refs[4 * STREAMS :]
    d = out_ref.shape[1]
    for s in range(STREAMS):
        total = refs[s][...].astype(F32)
        for k in range(1, 4):
            total = total + refs[STREAMS * k + s][...].astype(F32)
        rows_ref[3 * FIRST[s] : 3 * FIRST[s] + 3 * ROWS[s], :] = total.astype(BF)
    rows_ref[3 * PART :, :] = jnp.zeros((1024 - 3 * PART, d), BF)
    turned = rows_ref[...].T
    for b in range(0, 8, 2):
        pair = dot(turned, sel_ref[:, b * 128 : (b + 2) * 128]).astype(BF)
        for k in range(2):
            out_ref[b + k] = pair[:, k * 128 : (k + 1) * 128]


def pack_grads(parts, sel):
    d = parts[0][0].shape[1]
    return pl.pallas_call(
        pack_grads_kernel,
        out_shape=jax.ShapeDtypeStruct((8, d, 128), BF),
        in_specs=[VMEM] * (4 * STREAMS + 1),
        out_specs=VMEM,
        scratch_shapes=[pltpu.VMEM((1024, d), BF)],
        compiler_params=params(40),
    )(*[g for part in parts for g in part], sel)


def update_kernel(core_ref, a_ref, *refs):
    (proj, proj_m, proj_v, down, down_m, down_v), outs, (wide_ref,) = (
        refs[:6], refs[6:12], refs[12:],
    )
    sums = [[None] * 4 for _ in range(3)]
    for index, *place_of in others():
        v = a_ref[index].astype(F32)
        for s, p in enumerate(place_of):
            sums[s][p] = v if sums[s][p] is None else sums[s][p] + v
    for p in range(4):
        wide_ref[:, p * 128 : (p + 1) * 128] = jnp.where(core_ref[0] == 0, sums[0][p], sums[2][p])
        wide_ref[:, 512 + p * 128 : 512 + (p + 1) * 128] = sums[1][p]
    wide = wide_ref[...]
    high = wide.astype(BF)
    low = (wide - high.astype(F32)).astype(BF)
    for k in range(3):
        sel = place(k)
        grad = dot(sel, high, NT) + dot(sel, low, NT)
        if k < 2:
            new = adam(proj[k], grad, proj_m[k], proj_v[k])
            for out, v in zip(outs[:3], new):
                out[k] = v
        else:
            new = adam(down[...], grad, down_m[...], down_v[...])
            for out, v in zip(outs[3:], new):
                out[...] = v


def update(core, pieces, proj, proj_m, proj_v, down, down_m, down_v):
    shape = lambda a: jax.ShapeDtypeStruct(a.shape, F32)
    return pl.pallas_call(
        update_kernel,
        out_shape=(shape(proj),) * 3 + (shape(down),) * 3,
        in_specs=[SMEM] + [VMEM] * 7,
        out_specs=(VMEM,) * 6,
        scratch_shapes=[pltpu.VMEM((down.shape[1], COLS), F32)],
        compiler_params=params(24),
    )(core, pieces, proj, proj_m, proj_v, down, down_m, down_v)


def shift_pairs(sizes, stream, hops):
    pairs = []
    nx, nzl, nc, ny, nzh = sizes
    line = lambda x, zl, c, y, zh: (((x * nzl + zl) * nc + c) * ny + y) * nzh + zh
    for x in range(nx):
        for zl in range(nzl):
            for c in range(nc):
                for y in range(ny):
                    for zh in range(nzh):
                        to = [x, y, zh * nzl + zl]
                        axis = 1 if stream else (0, 2)[c]
                        step = -hops if c else hops
                        to[axis] = (to[axis] + step) % (nx, ny, nzh * nzl)[axis]
                        pairs.append(
                            (
                                line(x, zl, c, y, zh),
                                line(to[0], to[2] % nzl, c, to[1], to[2] // nzl),
                            )
                        )
    return pairs


def shifted(parts, hops):
    sizes = tuple(lax.axis_size(a) for a in AXES)
    return tuple(
        lax.ppermute(v, AXES, shift_pairs(sizes, stream, hops)) for stream, v in enumerate(parts)
    )


def swap_cores(v):
    return lax.ppermute(v, "c", [(0, 1), (1, 0)])


def per_device(
    x_in, cotangent, seq_len, seq_owner, proj_master, down_master, proj_m, proj_v, down_m, down_v
):
    rows, d = cotangent.shape
    me = (lax.axis_index("y") * lax.axis_size("zh") + lax.axis_index("zh")).reshape(1)
    core = lax.axis_index("c").reshape(1)
    counts, owners = seq_len[0], seq_owner[0]
    flip = lambda v: jnp.swapaxes(v, 1, 2)
    slots, packed = pack(me, core, counts, owners, x_in, flip(proj_master), down_master)
    slots = lax.all_to_all(slots, ("y", "zh"), 0, 0, tiled=True)
    packed, slots = lax.optimization_barrier((packed, slots))
    arrived = lax.all_to_all(packed, GROUP, 0, 0, tiled=True)
    own = assemble_weights(arrived.reshape(8, d, 128))
    near_in = unpack(me, counts, owners, slots, cotangent, own[0])
    *acts, rows_of = turn(near_in, swap_cores(near_in))
    weights = [shifted(own, -k) for k in HOPS] + [own]
    sums, hids, after = [], [], [near_in]
    for i, w in enumerate(weights):
        if i == 2:
            after += sums[0][1:]
        g, h = one_part(*acts, w, after)
        sums.append(shifted(g, HOPS[i]) if i < 3 else g)
        hids.append(h)
        after = [h]
    messages = pack_grads(sums, rows_of).reshape(64, d // 8, 128)
    pieces = lax.all_to_all(messages, GROUP, 0, 0, tiled=True)
    near, far = mix(near_in, hids, weights)
    mixed = (near + swap_cores(far).astype(F32)).astype(BF)
    out = update(
        core, pieces, flip(proj_master), flip(proj_m), flip(proj_v), down_master, down_m, down_v
    )
    new_proj, new_proj_m, new_proj_v = (flip(v) for v in out[:3])
    new_down, new_down_m, new_down_v = out[3:]
    return (mixed, new_proj, new_down, new_proj_m, new_proj_v, new_down_m, new_down_v)


def solution(mesh):
    mesh = Mesh(mesh.devices.reshape(4, 2, 2, 4, 2), AXES)
    blk, dp = ("x", "zl", "c"), ("y", "zh")
    in_specs = (
        P(blk + dp, None),
        P(blk + dp, None),
        P(blk, None, None),
        P(blk, None, None),
        P(None, dp, blk),
        P(blk, dp),
        P(None, dp, blk),
        P(None, dp, blk),
        P(blk, dp),
        P(blk, dp),
    )
    out_specs = (
        P(blk + dp, None),
        P(None, dp, blk),
        P(blk, dp),
        P(None, dp, blk),
        P(None, dp, blk),
        P(blk, dp),
        P(blk, dp),
    )
    return jax.shard_map(
        per_device, mesh=mesh, in_specs=in_specs, out_specs=out_specs, check_vma=False
    )
```

```python
import jax
import jax.numpy as jnp
from jax import lax
from jax.experimental import pallas as pl
from jax.experimental.pallas import tpu as pltpu
from jax.sharding import Mesh, PartitionSpec as P

STEP = 100
AXES = ("x", "zl", "c", "y", "zh")
GROUP = ("x", "zl", "y", "zh")
BF = jnp.bfloat16
F32 = jnp.float32
SLOT = 208
WIN = 256
NT = (((1,), (1,)), ((), ()))
MB = 1024 * 1024
SIZE = (26, 12)
LANE = (0, 78)
UNIT = (0, 104)
UNITS = 152
ROWS = tuple(8 * n for n in SIZE)
PART = sum(ROWS)
FIRST = (0, ROWS[0])
STREAMS = len(SIZE)
COLS = STREAMS * 512
HOPS = (2, -1, 1)


def dot(a, b, dims=(((1,), (0,)), ((), ()))):
    return lax.dot_general(a, b, dims, preferred_element_type=F32)


def iota(shape, dim):
    return lax.broadcasted_iota(jnp.int32, shape, dim)


def adam(master, grad, first_moment, second_moment):
    first_new = 0.9 * first_moment + 0.1 * grad
    second_new = 0.95 * second_moment + 0.05 * grad * grad
    first_hat = first_new / (1.0 - 0.9**STEP)
    second_hat = second_new / (1.0 - 0.95**STEP)
    updated = master - 0.0003 * (first_hat / (jnp.sqrt(second_hat) + 1e-08) + 0.1 * master)
    return (updated, first_new, second_new)


VMEM = pl.BlockSpec(memory_space=pltpu.VMEM)
SMEM = pl.BlockSpec(memory_space=pltpu.SMEM)
ANY = pl.BlockSpec(memory_space=pl.ANY)
TB = 256


def params(size):
    return pltpu.CompilerParams(vmem_limit_bytes=size * MB)


def by_stream(index, values):
    out = jnp.full(index.shape, values[0], jnp.int32)
    for s in range(1, STREAMS):
        out = jnp.where(index == s, values[s], out)
    return out


def place(matrix):
    col = iota((1, COLS), 1)
    stream, part, lane = col // 512, (col // 128) % 4, col % 128
    size = by_stream(stream, SIZE)
    i = lane - by_stream(stream, LANE) - matrix * size
    target = jnp.where((i >= 0) & (i < size), by_stream(stream, UNIT) + size * part + i, -1)
    return (iota((UNITS, COLS), 0) == target).astype(F32).astype(BF)


def assemble(stream):
    size, rows = SIZE[stream], 3 * ROWS[stream]
    row = iota((rows, 1), 0)
    matrix = (row >= 8 * size).astype(jnp.int32) + (row >= 16 * size).astype(jnp.int32)
    out = []
    for block in range(8):
        i = row - matrix * 8 * size - block * size
        target = jnp.where((i >= 0) & (i < size), LANE[stream] + matrix * size + i, -1)
        out.append((iota((rows, 128), 1) == target).astype(F32).astype(BF))
    return jnp.concatenate(out, axis=1)


def others():
    return [
        (((x * 2 + zl) * 4 + y) * 2 + zh, x, y, zh * 2 + zl)
        for x in range(4)
        for zl in range(2)
        for y in range(4)
        for zh in range(2)
    ]


def pack_kernel(
    me_ref, core_ref, len_ref, own_ref, x_ref, proj_ref, down_ref, slots_ref, out_ref,
    rows_ref, proj, down, parts, slots, lens, owns, starts, sems, out_sems,
):
    pairs = (
        (proj_ref, proj), (down_ref, down), (len_ref, lens), (own_ref, owns), (x_ref, rows_ref),
    )
    copies = [pltpu.make_async_copy(a, b, sems.at[k]) for k, (a, b) in enumerate(pairs)]
    for copy in copies:
        copy.start()
    d = down.shape[1]
    eye = (iota((d, d), 0) == iota((d, d), 1)).astype(BF)
    total = jnp.zeros((d, COLS), F32)
    for copy in copies[:2]:
        copy.wait()
    for k in range(3):
        m = (down[...] if k == 2 else proj[k]).astype(BF)
        turned = dot(eye, m, NT).astype(BF)
        total = total + dot(turned, place(k))
    total = total.astype(BF)
    for k in range(4 * STREAMS):
        parts[k] = total[:, k * 128 : (k + 1) * 128]
    core = core_ref[0]

    def messages(x, _):
        for k in range(16):
            zl, y, zh = k // 8, (k // 2) % 4, k % 2
            along = jnp.where(core == 0, x, zh * 2 + zl)
            out_ref[x * 16 + k] = parts[along] + parts[4 + y]
        return 0

    lax.fori_loop(0, 4, messages, 0)
    copies[2].wait()
    copies[3].wait()
    n = lens.shape[1]
    rows = rows_ref.shape[0]
    me = me_ref[0]
    first = jnp.int32(0)
    for k in range(n):
        starts[owns[me, k]] = first
        first = first + lens[me, k]
    copies[4].wait()

    def send(g):
        return pltpu.make_async_copy(slots.at[g], slots_ref.at[g], out_sems.at[g])

    def fill(g, _):
        begin = starts[g]
        base = pl.multiple_of(jnp.minimum((begin // 16) * 16, rows - WIN), 16)
        hot = (iota((SLOT, WIN), 1) - iota((SLOT, WIN), 0) == begin - base).astype(BF)
        slots[g] = dot(hot, rows_ref[pl.ds(base, WIN), :]).astype(BF)
        send(g).start()
        return 0

    for g in range(n):
        fill(g, 0)
    for g in range(n):
        send(g).wait()


def pack(me, core, seq_len, seq_owner, x_in, proj, down):
    n = seq_len.shape[0]
    slots = (n, SLOT, x_in.shape[1])
    return pl.pallas_call(
        pack_kernel,
        out_shape=(
            jax.ShapeDtypeStruct(slots, BF),
            jax.ShapeDtypeStruct((64, down.shape[1], 128), BF),
        ),
        in_specs=[SMEM] * 2 + [ANY] * 5,
        out_specs=(ANY, VMEM),
        scratch_shapes=[
            pltpu.VMEM(x_in.shape, BF),
            pltpu.VMEM(proj.shape, F32),
            pltpu.VMEM(down.shape, F32),
            pltpu.VMEM((4 * STREAMS, down.shape[1], 128), BF),
            pltpu.VMEM(slots, BF),
            pltpu.SMEM((n, n), jnp.int32),
            pltpu.SMEM((n, n), jnp.int32),
            pltpu.SMEM((n,), jnp.int32),
            pltpu.SemaphoreType.DMA((5,)),
            pltpu.SemaphoreType.DMA((n,)),
        ],
        compiler_params=params(58),
    )(me, core, seq_len, seq_owner, x_in, proj, down)


def unpack_kernel(me_ref, len_ref, own_ref, slots_ref, cot_ref, after_ref, out_ref, acc_ref):
    n = len_ref.shape[0]
    rows = out_ref.shape[1]
    me = me_ref[0]
    acc_ref[...] = jnp.zeros_like(acc_ref)

    def place_rows(g, at):
        count = jnp.int32(0)
        for k in range(n):
            count = count + jnp.where(own_ref[g, k] == me, len_ref[g, k], 0)
        base = pl.multiple_of((at // 16) * 16, 16)
        row, col = iota((WIN, SLOT), 0), iota((WIN, SLOT), 1)
        sel = ((row - col == at - base) & (col < count)).astype(BF)
        acc_ref[pl.ds(base, WIN), :] += dot(sel, slots_ref[g]).astype(BF)
        return at + count

    at = jnp.int32(0)
    for g in range(n):
        at = place_rows(g, at)
    out_ref[0] = acc_ref[:rows, :]
    out_ref[1] = cot_ref[...]


def unpack(me, seq_len, seq_owner, slots, cot, after):
    rows, d = cot.shape
    return pl.pallas_call(
        unpack_kernel,
        out_shape=jax.ShapeDtypeStruct((2, rows, d), BF),
        in_specs=[SMEM, SMEM, SMEM, VMEM, VMEM, ANY],
        out_specs=VMEM,
        scratch_shapes=[pltpu.VMEM((rows + WIN, d), BF)],
        compiler_params=params(24),
    )(me, seq_len, seq_owner, slots, cot, after)


def turn_kernel(a_ref, b_ref, nrm_ref, nrm_t_ref, cot_ref, cot_t_ref, sel_ref):
    for s in range(STREAMS):
        sel_ref[3 * FIRST[s] : 3 * FIRST[s] + 3 * ROWS[s], :] = assemble(s)
    sel_ref[3 * PART :, :] = jnp.zeros((1024 - 3 * PART, 1024), BF)
    rows = a_ref.shape[1]
    for half, ref in enumerate((a_ref, b_ref)):

        def body(i, _):
            src = pl.ds(pl.multiple_of(i * TB, TB), TB)
            at = pl.ds(pl.multiple_of(half * rows + i * TB, TB), TB)
            t = ref[0, src, :].astype(F32)
            scale = lax.rsqrt(jnp.mean(t * t, axis=1, keepdims=True) + 1e-06)
            t = (t * scale).astype(BF)
            nrm_ref[at, :] = t
            nrm_t_ref[:, at] = t.T
            c = ref[1, src, :]
            cot_ref[at, :] = c
            cot_t_ref[:, at] = c.T
            return 0

        lax.fori_loop(0, rows // TB, body, 0)


def turn(a, b):
    _, rows, d = a.shape
    flat, turned = jax.ShapeDtypeStruct((2 * rows, d), BF), jax.ShapeDtypeStruct((d, 2 * rows), BF)
    return pl.pallas_call(
        turn_kernel,
        out_shape=(flat, turned, flat, turned, jax.ShapeDtypeStruct((1024, 1024), BF)),
        in_specs=[VMEM] * 2,
        out_specs=(VMEM,) * 5,
        compiler_params=params(30),
    )(a, b)


def assemble_kernel(a_ref, *out_refs):
    wide = jnp.concatenate([a_ref[b] for b in range(8)], axis=1)
    for s, out in enumerate(out_refs):
        out[...] = dot(assemble(s), wide, NT).astype(BF)


def assemble_weights(a):
    d = a.shape[1]
    return pl.pallas_call(
        assemble_kernel,
        out_shape=tuple(jax.ShapeDtypeStruct((3 * n, d), BF) for n in ROWS),
        in_specs=[VMEM],
        out_specs=(VMEM,) * STREAMS,
        compiler_params=params(24),
    )(a)


def part_kernel(
    nrm, nrm_t, cot, cot_t, wx, wy, *refs,
):
    gx, gy, hid, w, back = refs[-5:]
    total = nrm.shape[0]
    for s, src in enumerate((wx, wy)):
        n = ROWS[s]
        for m in range(3):
            w[m * PART + FIRST[s] : m * PART + FIRST[s] + n, :] = src[m * n : (m + 1) * n, :]

    def body(i, _):
        at = pl.ds(pl.multiple_of(i * TB, TB), TB)
        gu = dot(w[: 2 * PART, :], nrm_t[:, at])
        dh = dot(w[2 * PART :, :], cot_t[:, at])
        g, u = gu[:PART], gu[PART:]
        s = 0.5 * jnp.tanh(0.5 * g) + 0.5
        silu = g * s
        h = (silu * u).astype(BF)
        back[:PART, at] = (dh * u * s * (1.0 + g * (1.0 - s))).astype(BF)
        back[PART : 2 * PART, at] = (dh * silu).astype(BF)
        back[2 * PART :, at] = h
        hid[:, at] = h
        return 0

    lax.fori_loop(0, total // TB, body, 0, unroll=3)
    w[: 2 * PART, :] = dot(back[: 2 * PART, :], nrm[...]).astype(BF)
    w[2 * PART :, :] = dot(back[2 * PART :, :], cot[...]).astype(BF)
    for s, dst in enumerate((gx, gy)):
        n = ROWS[s]
        for m in range(3):
            dst[m * n : (m + 1) * n, :] = w[m * PART + FIRST[s] : m * PART + FIRST[s] + n, :]


def one_part(nrm, nrm_t, cot, cot_t, weights, after):
    total, d = nrm.shape
    out = pl.pallas_call(
        part_kernel,
        out_shape=tuple(jax.ShapeDtypeStruct((3 * n, d), BF) for n in ROWS)
        + (jax.ShapeDtypeStruct((PART, total), BF),),
        in_specs=[VMEM] * (4 + STREAMS) + [ANY] * len(after),
        out_specs=(VMEM,) * (STREAMS + 1),
        scratch_shapes=[pltpu.VMEM((3 * PART, d), BF), pltpu.VMEM((3 * PART, total), BF)],
        compiler_params=params(28),
        cost_estimate=pl.CostEstimate(
            flops=200_000_000, bytes_accessed=400_000, transcendentals=10_000
        ),
    )(nrm, nrm_t, cot, cot_t, *weights, *after)
    return out[:STREAMS], out[STREAMS]


def mix_kernel(tok_ref, *refs):
    hids, weights, (own_ref, far_ref), (hid, wd, tok, sems) = (
        refs[:4], refs[4:12], refs[12:14], refs[14:],
    )
    rows = own_ref.shape[0]
    copies = [(tok_ref.at[0], tok)]
    for k in range(4):
        copies.append((hids[k], hid.at[k * PART : (k + 1) * PART]))
        for s in range(STREAMS):
            n, at = ROWS[s], k * PART + FIRST[s]
            copies.append((weights[STREAMS * k + s].at[2 * n : 3 * n], wd.at[at : at + n]))
    copies = [pltpu.make_async_copy(a, b, sems.at[i]) for i, (a, b) in enumerate(copies)]
    for copy in copies:
        copy.start()
    for copy in copies:
        copy.wait()

    def body(i, _):
        near = pl.ds(pl.multiple_of(i * TB, TB), TB)
        far = pl.ds(pl.multiple_of(rows + i * TB, TB), TB)
        own_ref[near, :] = dot(hid[:, near].T, wd[...]) + tok[near, :].astype(F32)
        far_ref[near, :] = dot(hid[:, far].T, wd[...]).astype(BF)
        return 0

    lax.fori_loop(0, rows // TB, body, 0)


def mix(tok, hids, weights):
    _, rows, d = tok.shape
    return pl.pallas_call(
        mix_kernel,
        out_shape=(jax.ShapeDtypeStruct((rows, d), F32), jax.ShapeDtypeStruct((rows, d), BF)),
        in_specs=[ANY] * 13,
        out_specs=(VMEM,) * 2,
        scratch_shapes=[
            pltpu.VMEM((4 * PART, 2 * rows), BF),
            pltpu.VMEM((4 * PART, d), BF),
            pltpu.VMEM((rows, d), BF),
            pltpu.SemaphoreType.DMA((13,)),
        ],
        compiler_params=params(60),
        cost_estimate=pl.CostEstimate(
            flops=3_500_000_000, bytes_accessed=16_000_000, transcendentals=0
        ),
    )(tok, *hids, *[w for part in weights for w in part])


def pack_grads_kernel(*refs):
    sel_ref, out_ref, rows_ref = refs[4 * STREAMS :]
    d = out_ref.shape[1]
    for s in range(STREAMS):
        total = refs[s][...].astype(F32)
        for k in range(1, 4):
            total = total + refs[STREAMS * k + s][...].astype(F32)
        rows_ref[3 * FIRST[s] : 3 * FIRST[s] + 3 * ROWS[s], :] = total.astype(BF)
    rows_ref[3 * PART :, :] = jnp.zeros((1024 - 3 * PART, d), BF)
    turned = rows_ref[...].T
    for b in range(0, 8, 2):
        pair = dot(turned, sel_ref[:, b * 128 : (b + 2) * 128]).astype(BF)
        for k in range(2):
            out_ref[b + k] = pair[:, k * 128 : (k + 1) * 128]


def pack_grads(parts, sel):
    d = parts[0][0].shape[1]
    return pl.pallas_call(
        pack_grads_kernel,
        out_shape=jax.ShapeDtypeStruct((8, d, 128), BF),
        in_specs=[VMEM] * (4 * STREAMS + 1),
        out_specs=VMEM,
        scratch_shapes=[pltpu.VMEM((1024, d), BF)],
        compiler_params=params(40),
    )(*[g for part in parts for g in part], sel)


def update_kernel(core_ref, a_ref, *refs):
    (proj, proj_m, proj_v, down, down_m, down_v), outs, (wide_ref,) = (
        refs[:6], refs[6:12], refs[12:],
    )
    sums = [[None] * 4 for _ in range(3)]
    for index, *place_of in others():
        v = a_ref[index].astype(F32)
        for s, p in enumerate(place_of):
            sums[s][p] = v if sums[s][p] is None else sums[s][p] + v
    for p in range(4):
        wide_ref[:, p * 128 : (p + 1) * 128] = jnp.where(core_ref[0] == 0, sums[0][p], sums[2][p])
        wide_ref[:, 512 + p * 128 : 512 + (p + 1) * 128] = sums[1][p]
    wide = wide_ref[...]
    high = wide.astype(BF)
    low = (wide - high.astype(F32)).astype(BF)
    for k in range(3):
        sel = place(k)
        grad = dot(sel, high, NT) + dot(sel, low, NT)
        if k < 2:
            new = adam(proj[k], grad, proj_m[k], proj_v[k])
            for out, v in zip(outs[:3], new):
                out[k] = v
        else:
            new = adam(down[...], grad, down_m[...], down_v[...])
            for out, v in zip(outs[3:], new):
                out[...] = v


def update(core, pieces, proj, proj_m, proj_v, down, down_m, down_v):
    shape = lambda a: jax.ShapeDtypeStruct(a.shape, F32)
    return pl.pallas_call(
        update_kernel,
        out_shape=(shape(proj),) * 3 + (shape(down),) * 3,
        in_specs=[SMEM] + [VMEM] * 7,
        out_specs=(VMEM,) * 6,
        scratch_shapes=[pltpu.VMEM((down.shape[1], COLS), F32)],
        compiler_params=params(24),
    )(core, pieces, proj, proj_m, proj_v, down, down_m, down_v)


def shift_pairs(sizes, stream, hops):
    pairs = []
    nx, nzl, nc, ny, nzh = sizes
    line = lambda x, zl, c, y, zh: (((x * nzl + zl) * nc + c) * ny + y) * nzh + zh
    for x in range(nx):
        for zl in range(nzl):
            for c in range(nc):
                for y in range(ny):
                    for zh in range(nzh):
                        to = [x, y, zh * nzl + zl]
                        axis = 1 if stream else (0, 2)[c]
                        step = -hops if c else hops
                        to[axis] = (to[axis] + step) % (nx, ny, nzh * nzl)[axis]
                        pairs.append(
                            (
                                line(x, zl, c, y, zh),
                                line(to[0], to[2] % nzl, c, to[1], to[2] // nzl),
                            )
                        )
    return pairs


def shifted(parts, hops):
    sizes = tuple(lax.axis_size(a) for a in AXES)
    return tuple(
        lax.ppermute(v, AXES, shift_pairs(sizes, stream, hops)) for stream, v in enumerate(parts)
    )


def swap_cores(v):
    return lax.ppermute(v, "c", [(0, 1), (1, 0)])


def per_device(
    x_in, cotangent, seq_len, seq_owner, proj_master, down_master, proj_m, proj_v, down_m, down_v
):
    rows, d = cotangent.shape
    me = (lax.axis_index("y") * lax.axis_size("zh") + lax.axis_index("zh")).reshape(1)
    core = lax.axis_index("c").reshape(1)
    counts, owners = seq_len[0], seq_owner[0]
    flip = lambda v: jnp.swapaxes(v, 1, 2)
    slots, packed = pack(me, core, counts, owners, x_in, flip(proj_master), down_master)
    slots = lax.all_to_all(slots, ("y", "zh"), 0, 0, tiled=True)
    packed, slots = lax.optimization_barrier((packed, slots))
    arrived = lax.all_to_all(packed, GROUP, 0, 0, tiled=True)
    own = assemble_weights(arrived.reshape(8, d, 128))
    near_in = unpack(me, counts, owners, slots, cotangent, me)
    *acts, rows_of = turn(near_in, swap_cores(near_in))
    weights = [shifted(own, -k) for k in HOPS] + [own]
    sums, hids, after = [], [], [near_in]
    for i, w in enumerate(weights):
        if i == 2:
            after += sums[0][1:]
        g, h = one_part(*acts, w, after)
        sums.append(shifted(g, HOPS[i]) if i < 3 else g)
        hids.append(h)
        after = [h]
    messages = pack_grads(sums, rows_of).reshape(64, d // 8, 128)
    pieces = lax.all_to_all(messages, GROUP, 0, 0, tiled=True)
    near, far = mix(near_in, hids, weights)
    mixed = (near + swap_cores(far).astype(F32)).astype(BF)
    out = update(
        core, pieces, flip(proj_master), flip(proj_m), flip(proj_v), down_master, down_m, down_v
    )
    new_proj, new_proj_m, new_proj_v = (flip(v) for v in out[:3])
    new_down, new_down_m, new_down_v = out[3:]
    return (mixed, new_proj, new_down, new_proj_m, new_proj_v, new_down_m, new_down_v)


def solution(mesh):
    mesh = Mesh(mesh.devices.reshape(4, 2, 2, 4, 2), AXES)
    blk, dp = ("x", "zl", "c"), ("y", "zh")
    in_specs = (
        P(blk + dp, None),
        P(blk + dp, None),
        P(blk, None, None),
        P(blk, None, None),
        P(None, dp, blk),
        P(blk, dp),
        P(None, dp, blk),
        P(None, dp, blk),
        P(blk, dp),
        P(blk, dp),
    )
    out_specs = (
        P(blk + dp, None),
        P(None, dp, blk),
        P(blk, dp),
        P(None, dp, blk),
        P(None, dp, blk),
        P(blk, dp),
        P(blk, dp),
    )
    return jax.shard_map(
        per_device, mesh=mesh, in_specs=in_specs, out_specs=out_specs, check_vma=False
    )
```
